128 devices in a mesh: seq: 8 (over x_lo, z), chan: 16 (over x_hi, y, core).
Axes of the slice: x: 4 (x_hi: 2, x_lo: 2; x = x_hi * 2 + x_lo), y: 4, z: 4, core: 2. Of those that a mesh axis runs over, the one named last changes fastest.
Arguments:
- projections: bfloat16 [3, 256, 32768], P(None, None, ('seq', 'chan')), may hold values from -6 to 6
- taps: float32 [3, 256, 3], replicated, may hold values from -2.4 to 2.4
- filter_spectra: float32 [256, 64, 2, 1024], P('chan'), may hold values from -1.2 to 1.2
- skip_gain: float32 [256], replicated, may hold values from -3 to 3
Outputs:
- gated: bfloat16 [256, 32768], P('chan', 'seq')
The draws below stay inside these ranges and needn't reach their ends.
All inputs are finite; a program needn't handle non-finite values.
Results may differ from the reference program's by a relative error of at most 0.001.
Values may be sent and summed in bfloat16 or wider, within the bound.
No kernel may reach another device: no remote copies, remote signals or barrier semaphores. Data moves between devices by JAX's collectives and lax.ppermute only.
A program may use at most 64 MiB of HBM per device.

```python
import jax
import jax.numpy as jnp
from jax import lax

C = 256
TAPS = 3
SUB = 512
LENGTH = 32768
LAGS = 64
FREQ = 1024


def levels(key, shape, split, low, largest):
    gain, own = 1.0, jax.random.fold_in(key, 6)
    for dim, blocks in split:
        steps = jnp.exp(jax.random.uniform(jax.random.fold_in(own, dim), (blocks,), jnp.float32, low / len(split), largest / len(split)))
        gain = gain * jnp.repeat(steps, shape[dim] // blocks).reshape([-1 if axis == dim else 1 for axis in range(len(shape))])
    return gain


def normal_values(own_key, dims, width, limit, shards=(), held_as=jnp.bfloat16):
    values = width * jax.random.normal(own_key, dims, jnp.float32)
    if shards:
        values = values * levels(own_key, dims, shards, -0.22, 0.18)
    return jnp.clip(values, -limit, limit).astype(held_as)


def setup_inputs(seed: int = 0) -> dict:
    arg_keys = jax.random.split(jax.random.key(seed), 5)
    projections = normal_values(arg_keys[0], (3, C, LENGTH), 1.0, 6.0, ((2, 128),))
    taps = normal_values(arg_keys[1], (3, C, TAPS), 0.4, 2.4, (), jnp.float32)
    filter_spectra = normal_values(arg_keys[2], (C, LAGS, 2, FREQ), 0.2, 1.2, ((0, 16),), jnp.float32)
    skip_gain = normal_values(arg_keys[3], (C,), 0.5, 3.0, (), jnp.float32)
    return dict(projections=projections, taps=taps, filter_spectra=filter_spectra, skip_gain=skip_gain)


def featurize(projections, taps):
    rows = projections.astype(jnp.float32)
    edge = TAPS - 1
    padded = jnp.pad(rows, ((0, 0), (0, 0), (edge, 0)))
    total = jnp.zeros(rows.shape, jnp.float32)
    for shift_at in range(TAPS):
        total = total + taps[:, :, shift_at:shift_at + 1] * padded[:, :, edge - shift_at:edge - shift_at + LENGTH]
    return total


def reference(projections, taps, filter_spectra, skip_gain):
    features = featurize(projections, taps)
    query, key, value = features[0], features[1], features[2]
    product = key * value
    blocks_all = product.reshape(C, LAGS, SUB)
    spectrum = jnp.fft.fft(blocks_all, n=FREQ, axis=-1)
    filters = lax.complex(filter_spectra[:, :, 0, :], filter_spectra[:, :, 1, :])
    mixed = jnp.fft.ifft(jnp.fft.fft(filters, n=2 * LAGS, axis=1) * jnp.fft.fft(spectrum, n=2 * LAGS, axis=1), axis=1)[:, :LAGS]
    long_part = jnp.real(jnp.fft.ifft(mixed, axis=-1))[:, :, :SUB].reshape(C, LENGTH)
    return (query * (long_part + skip_gain[:, None] * product)).astype(jnp.bfloat16)
```

```python
import math

import jax
import jax.numpy as jnp
import numpy as np
from jax import lax
from jax.sharding import PartitionSpec as P

HIGH = lax.Precision.HIGH


def tables(sub, lags):
    freq = 2 * sub
    width = sub + 128
    s = np.arange(sub)[:, None]
    f = np.arange(width)[None, :]
    angle = 2 * np.pi * ((s * f) % freq) / freq
    keep = (f <= sub).astype(np.float64)
    weight = np.where((f == 0) | (f == sub), 1.0, 2.0) * keep / freq
    cos, sin = np.cos(angle), np.sin(angle)
    forward = np.concatenate([cos * keep, -sin * keep], axis=1)
    inverse = np.concatenate([(cos * weight).T, (-sin * weight).T], axis=0)
    turns = 2 * lags
    k = np.arange(turns)[:, None]
    p = np.arange(lags)[None, :]
    theta = 2 * np.pi * ((k * p) % turns) / turns
    c, sn = np.cos(theta), np.sin(theta)
    across = np.block([[c, sn], [-sn, c]])
    back = np.block([[c.T, -sn.T], [sn.T, c.T]]) / turns
    return [np.asarray(t, np.float32) for t in (forward, inverse, across, back)]


def body(projections, taps, filter_spectra, skip_gain):
    chan_count, seq_count = lax.axis_size("chan"), lax.axis_size("seq")
    count = chan_count * seq_count
    streams, channels, tokens = projections.shape
    mine = channels // count
    length = tokens * count
    lags = filter_spectra.shape[1]
    sub = filter_spectra.shape[3] // 2
    local = filter_spectra.shape[0]
    forward, inverse, across, back = (jnp.asarray(t) for t in tables(sub, lags))
    within = lax.axis_index("seq") * mine
    offset = lax.axis_index("chan") * local + within
    my_taps = lax.dynamic_slice_in_dim(taps, offset, mine, 1)
    my_gain = lax.dynamic_slice_in_dim(skip_gain, offset, mine, 0)
    my_filter = lax.dynamic_slice_in_dim(filter_spectra, within, mine, 0)

    sent = projections.reshape(streams, count, mine, tokens)
    got = lax.all_to_all(sent, ("chan", "seq"), 1, 1, tiled=True)
    got = got.reshape(streams, chan_count, seq_count, mine, tokens)
    rows = got.transpose(0, 3, 2, 1, 4).reshape(streams, mine, length).astype(jnp.float32)
    edge = taps.shape[2] - 1
    padded = jnp.pad(rows, ((0, 0), (0, 0), (edge, 0)))
    features = sum(
        my_taps[:, :, i : i + 1] * padded[:, :, edge - i : edge - i + length] for i in range(edge + 1)
    )
    query, key, value = features[0], features[1], features[2]
    product = key * value

    g = my_filter[:, :, :, : sub + 1]
    mirror = jnp.concatenate([my_filter[:, :, :, :1], my_filter[:, :, :, sub:][:, :, :, ::-1]], axis=3)
    flip = jnp.array([0.5, -0.5], jnp.float32)[:, None]
    herm = jnp.pad(0.5 * g + flip * mirror, ((0, 0), (0, 0), (0, 0), (0, 127)))
    herm = herm.transpose(0, 2, 1, 3).reshape(mine, 2 * lags, sub + 128)
    ghat = jnp.einsum("kp,cpf->ckf", across, herm, precision=HIGH)

    spec = jnp.einsum("cps,sf->cpf", product.reshape(mine, lags, sub), forward, precision=HIGH)
    spec = spec.reshape(mine, lags, 2, sub + 128).transpose(0, 2, 1, 3).reshape(mine, 2 * lags, sub + 128)
    xhat = jnp.einsum("kp,cpf->ckf", across, spec, precision=HIGH)
    turns = 2 * lags
    gr, gi, xr, xi = ghat[:, :turns], ghat[:, turns:], xhat[:, :turns], xhat[:, turns:]
    yhat = jnp.concatenate([gr * xr - gi * xi, gr * xi + gi * xr], axis=1)
    mixed = jnp.einsum("nk,ckf->cnf", back, yhat, precision=HIGH)
    mixed = mixed.reshape(mine, 2, lags, sub + 128).transpose(0, 2, 1, 3).reshape(mine, lags, 2 * sub + 256)
    long_part = jnp.einsum("cnf,fs->cns", mixed, inverse, precision=HIGH).reshape(mine, length)
    out = (query * (long_part + my_gain[:, None] * product)).astype(jnp.bfloat16)
    out = out.reshape(mine, seq_count, length // seq_count).transpose(1, 0, 2)
    out = lax.all_to_all(out, "seq", 0, 0, tiled=True)
    return out.reshape(local, length // seq_count)


def solution(mesh):
    placed = (P(None, None, ("seq", "chan")), P(), P("chan", None, None, None), P())
    return jax.shard_map(
        body, mesh=mesh, in_specs=placed, out_specs=P("chan", "seq"), check_vma=False
    )
```

```python
import math

import jax
import jax.numpy as jnp
import numpy as np
from jax import lax
from jax.experimental import pallas as pl
from jax.experimental.pallas import tpu as pltpu
from jax.sharding import PartitionSpec as P

F32, BF16 = jnp.float32, jnp.bfloat16


def halves(x):
    high = x.astype(BF16)
    return high, (x - high.astype(F32)).astype(BF16)


def table(x):
    high = np.asarray(x, np.float32).astype(BF16)
    low = (np.asarray(x, np.float64) - high.astype(np.float64)).astype(BF16)
    return jnp.asarray(high), jnp.asarray(low)


def dot(a, b):
    return jnp.dot(a, b, preferred_element_type=F32)


def dot_t(a, b):
    return lax.dot_general(a, b, (((1,), (1,)), ((), ())), preferred_element_type=F32)


def block_table(sub, width):
    freq = 2 * sub
    s = np.arange(sub)[:, None]
    f = np.arange(width)[None, :]
    angle = 2 * np.pi * ((s * f) % freq) / freq
    keep = f <= sub
    return np.concatenate([np.cos(angle) * keep, -np.sin(angle) * keep], axis=1)


def lag_tables(lags):
    turns = 2 * lags
    k = np.arange(turns)[:, None]
    p = np.arange(lags)[None, :]
    theta = 2 * np.pi * ((k * p) % turns) / turns
    c, sn = np.cos(theta), np.sin(theta)
    across = np.block([[c, sn], [-sn, c]])
    woven = across.reshape(2 * turns, 2, lags).transpose(0, 2, 1).reshape(2 * turns, 2 * lags)
    back = np.block([[c.T, -sn.T], [sn.T, c.T]]) / turns
    return across, woven, back


def filter_kernel(g_ref, high_ref, low_ref, out_ref):
    mine, rows, freq = g_ref.shape
    tiles = freq // 128
    lane = lax.broadcasted_iota(jnp.int32, (rows, 128), 1)
    row = lax.broadcasted_iota(jnp.int32, (rows, 128), 0)
    sign = jnp.where(row % 2 == 0, 1.0, -1.0).astype(F32)
    behind = (128 - lane) % 128
    for r in range(mine):
        parts = []
        for t in range(tiles // 2):
            here = g_ref[r, :, t * 128 : t * 128 + 128]
            far = g_ref[r, :, freq - t * 128 - 128 : freq - t * 128]
            edge = (tiles - t) % tiles
            first = g_ref[r, :, edge * 128 : edge * 128 + 128]
            mirror = jnp.where(lane == 0, first, jnp.take_along_axis(far, behind, axis=1))
            scale = jnp.where((lane == 0) & (t == 0), 0.5 / freq, 1.0 / freq).astype(F32)
            parts.append((here + sign * mirror) * scale)
        half = g_ref[r, :, freq // 2 : freq // 2 + 128]
        parts.append(jnp.where(lane == 0, (half + sign * half) * (0.5 / freq), 0.0))
        high, low = halves(jnp.concatenate(parts, axis=1))
        out_ref[r] = dot(high_ref[...], high) + dot(high_ref[...], low) + dot(low_ref[...], high)


def shifted(pair, by, lane, first_row):
    turned = [pltpu.roll(x, by, 1) for x in pair]
    down = jnp.where(first_row, 0.0, pltpu.roll(turned[1][:, :128], 1, 0))
    inner = [down, turned[0][:, :128]]
    return [
        jnp.concatenate([jnp.where(lane < by, inner[h], turned[h][:, :128]), turned[h][:, 128:]], axis=1)
        for h in range(2)
    ]


def main_kernel(scal_ref, rows_ref, ghat_ref, wh_ref, wl_ref, ah_ref, al_ref, bh_ref, bl_ref, out_ref):
    streams, mine, two, lags, chunk = rows_ref.shape
    width = ghat_ref.shape[2]
    turns = 2 * lags
    lane = lax.broadcasted_iota(jnp.int32, (lags, 128), 1)
    first_row = lax.broadcasted_iota(jnp.int32, (lags, 128), 0) == 0
    features = []
    for g in range(streams):
        per = []
        for r in range(mine):
            pair = [rows_ref[g, r, h] for h in range(2)]
            one, two_back = shifted(pair, 1, lane, first_row), shifted(pair, 2, lane, first_row)
            t = [scal_ref[(g * mine + r) * 3 + i] for i in range(3)]
            per.append(
                jnp.concatenate([t[0] * pair[h] + t[1] * one[h] + t[2] * two_back[h] for h in range(2)], axis=1)
            )
        features.append(per)
    product = [features[1][r] * features[2][r] for r in range(mine)]
    high, low = halves(jnp.concatenate(product, axis=0))
    spec = dot(high, wh_ref[...]) + dot(low, wh_ref[...]) + dot(high, wl_ref[...])
    mixed = []
    for r in range(mine):
        mine_spec = spec[r * lags : (r + 1) * lags]
        zh, zl = halves(jnp.concatenate([mine_spec[:, :width], mine_spec[:, width:]], axis=0))
        xhat = dot(ah_ref[...], zh) + dot(ah_ref[...], zl) + dot(al_ref[...], zh)
        xr, xi = xhat[:turns], xhat[turns:]
        gr, gi = ghat_ref[r, :turns], ghat_ref[r, turns:]
        yh, yl = halves(jnp.concatenate([gr * xr - gi * xi, gr * xi + gi * xr], axis=0))
        m = dot(bh_ref[...], yh) + dot(bh_ref[...], yl) + dot(bl_ref[...], yh)
        mixed.append(jnp.concatenate([m[:lags], m[lags:]], axis=1))
    mh, ml = halves(jnp.concatenate(mixed, axis=0))
    long_part = dot_t(mh, wh_ref[...]) + dot_t(ml, wh_ref[...]) + dot_t(mh, wl_ref[...])
    for r in range(mine):
        gain = scal_ref[streams * mine * 3 + r]
        out_ref[r] = features[0][r] * (long_part[r * lags : (r + 1) * lags] + gain * product[r])


def body(projections, taps, filter_spectra, skip_gain):
    chan_count, seq_count = lax.axis_size("chan"), lax.axis_size("seq")
    count = chan_count * seq_count
    streams, channels, tokens = projections.shape
    mine = channels // count
    length = tokens * count
    lags = filter_spectra.shape[1]
    freq = filter_spectra.shape[3]
    sub = freq // 2
    width = sub + 128
    local = filter_spectra.shape[0]
    wh, wl = table(block_table(sub, width))
    across, woven, back = lag_tables(lags)
    ah, al = table(across)
    vh, vl = table(woven)
    bh, bl = table(back)
    within = lax.axis_index("seq") * mine
    offset = lax.axis_index("chan") * local + within
    my_taps = lax.dynamic_slice_in_dim(taps, offset, mine, 1)
    my_gain = lax.dynamic_slice_in_dim(skip_gain, offset, mine, 0)
    scalars = jnp.concatenate([my_taps.reshape(-1), my_gain])
    my_filter = lax.dynamic_slice_in_dim(filter_spectra, within, mine, 0)
    vmem, smem = pl.BlockSpec(memory_space=pltpu.VMEM), pl.BlockSpec(memory_space=pltpu.SMEM)

    got = lax.all_to_all(projections, ("chan", "seq"), 1, 1, tiled=True)
    ghat = pl.pallas_call(
        filter_kernel,
        out_shape=jax.ShapeDtypeStruct((mine, 4 * lags, width), F32),
        in_specs=[vmem] * 3,
        out_specs=vmem,
        compiler_params=pltpu.CompilerParams(vmem_limit_bytes=16 << 20),
        cost_estimate=pl.CostEstimate(flops=3 * 2 * mine * 4 * lags * 2 * lags * width, bytes_accessed=4 << 20, transcendentals=0),
    )(my_filter.reshape(mine, 2 * lags, freq), vh, vl)
    per = sub // tokens
    got = got.reshape(streams, chan_count // per, per, seq_count, mine, tokens)
    rows = got.transpose(0, 4, 2, 3, 1, 5).reshape(streams, mine, per, lags, tokens).astype(F32)
    out = pl.pallas_call(
        main_kernel,
        out_shape=jax.ShapeDtypeStruct((mine, lags, sub), F32),
        in_specs=[smem] + [vmem] * 8,
        out_specs=vmem,
        compiler_params=pltpu.CompilerParams(vmem_limit_bytes=24 << 20),
        cost_estimate=pl.CostEstimate(flops=1 << 30, bytes_accessed=8 << 20, transcendentals=0),
    )(scalars, rows, ghat, wh, wl, ah, al, bh, bl)
    out = out.astype(BF16).reshape(mine, seq_count, length // seq_count).transpose(1, 0, 2)
    out = lax.all_to_all(out, "seq", 0, 0, tiled=True)
    return out.reshape(local, length // seq_count)


def solution(mesh):
    placed = (P(None, None, ("seq", "chan")), P(), P("chan", None, None, None), P())
    return jax.shard_map(
        body, mesh=mesh, in_specs=placed, out_specs=P("chan", "seq"), check_vma=False
    )
```

```python
import jax
import jax.numpy as jnp
import numpy as np
from jax import lax
from jax.experimental import pallas as pl
from jax.experimental.pallas import tpu as pltpu
from jax.sharding import PartitionSpec as P

F32, BF16 = jnp.float32, jnp.bfloat16


def halves(x):
    high = x.astype(BF16)
    return high, (x - high.astype(F32)).astype(BF16)


def table(x):
    high = np.asarray(x, np.float32).astype(BF16)
    low = (np.asarray(x, np.float64) - high.astype(np.float64)).astype(BF16)
    return high, low


def dot(a, b):
    return jnp.dot(a, b, preferred_element_type=F32)


def fixed(x):
    return pltpu.with_memory_space_constraint(jnp.asarray(x), pltpu.HBM)


def join(parts, axis):
    return jnp.concatenate(parts, axis=axis)


def block_tables(sub):
    freq = 2 * sub
    s = np.arange(sub)[:, None]
    f = np.arange(sub)[None, :]
    angle = 2 * np.pi * ((s * f) % freq) / freq
    imag = -np.sin(angle)
    imag[:, 0] = 1.0 - 2.0 * (np.arange(sub) % 2)
    forward = np.concatenate([np.cos(angle), imag], axis=1)
    return forward, np.ascontiguousarray(forward.T)


def lag_tables(lags, order):
    turns = 2 * lags
    k = np.arange(turns)[:, None]

    def turn(p):
        theta = 2 * np.pi * ((k * p[None, :]) % turns) / turns
        c, sn = np.cos(theta), np.sin(theta)
        return c, sn, np.block([[c, sn], [-sn, c]])

    woven = turn(np.arange(lags))[2]
    woven = woven.reshape(2 * turns, 2, lags).transpose(0, 2, 1).reshape(2 * turns, 2 * lags)
    c, sn, across = turn(order)
    back = np.block([[c.T, -sn.T], [sn.T, c.T]]) / turns
    return across, woven, back


def send_kernel(x_ref, out_ref, x_buf, out_buf, in_sem, out_sem):
    count, streams, mine, tokens = out_ref.shape
    reads = [pltpu.make_async_copy(x_ref.at[g], x_buf.at[g], in_sem.at[g]) for g in range(streams)]
    for read in reads:
        read.start()
    for g in range(streams):
        reads[g].wait()
        out_buf[:, g] = x_buf[g].reshape(count, mine, tokens)
    write = pltpu.make_async_copy(out_buf, out_ref, out_sem)
    write.start()
    write.wait()


def filter_kernel(g_hbm, taps_hbm, gain_hbm, lag_hbm, *refs):
    tables_hbm, out_ref, scal_ref, tables_ref = refs[:3], refs[3], refs[4], refs[5:8]
    g_ref, taps_ref, gain_ref, lag_ref, sems = refs[8:]
    mine, lags, two, freq = g_ref.shape
    local = g_hbm.shape[0]
    rows = lags * two
    tiles = freq // 128
    place = lax.axis_index("seq") * mine
    offset = lax.axis_index("chan") * local + place
    copies = [
        pltpu.make_async_copy(g_hbm.at[pl.ds(place, mine)], g_ref, sems.at[0]),
        pltpu.make_async_copy(lag_hbm, lag_ref, sems.at[1]),
        pltpu.make_async_copy(taps_hbm, taps_ref, sems.at[2]),
        pltpu.make_async_copy(gain_hbm, gain_ref, sems.at[3]),
    ]
    copies += [pltpu.make_async_copy(tables_hbm[k], tables_ref[k], sems.at[4 + k]) for k in range(3)]
    for copy in copies:
        copy.start()
    copies[3].wait()
    copies[2].wait()
    streams, edge_taps, channels = taps_ref.shape
    at = lax.broadcasted_iota(jnp.int32, (edge_taps, channels), 1)
    odd = lax.broadcasted_iota(jnp.int32, scal_ref.shape[1:], 0) % 2 == 1

    def pick(x, r):
        hit = lax.broadcasted_iota(jnp.int32, x.shape, 1) == offset + r
        return jnp.sum(jnp.where(hit, x, 0.0), axis=1, keepdims=True)

    for g in range(streams):
        even, second = (pick(taps_ref[g], r) for r in range(2))
        for i in range(edge_taps):
            scal_ref[g * edge_taps + i] = jnp.where(odd, second[i : i + 1], even[i : i + 1])
    even, second = (pick(gain_ref[...], r) for r in range(2))
    scal_ref[streams * edge_taps] = jnp.where(odd, second, even)

    lane = lax.broadcasted_iota(jnp.int32, (rows, 128), 1)
    row = lax.broadcasted_iota(jnp.int32, (rows, 128), 0)
    sign = jnp.where(row % 2 == 0, 1.0, -1.0).astype(F32)
    behind = (128 - lane) % 128
    copies[1].wait()
    copies[0].wait()
    wide = 2 * rows
    gh, gl = lag_ref[:wide], lag_ref[wide:]
    for r in range(mine):
        g = g_ref[r].reshape(rows, freq)
        parts = []
        for t in range(tiles // 2):
            here = g[:, t * 128 : t * 128 + 128]
            far = g[:, freq - t * 128 - 128 : freq - t * 128]
            edge = (tiles - t) % tiles
            first = g[:, edge * 128 : edge * 128 + 128]
            mirror = jnp.where(lane == 0, first, jnp.take_along_axis(far, behind, axis=1))
            scale = jnp.where((lane == 0) & (t == 0), 0.5 / freq, 1.0 / freq).astype(F32)
            parts.append((here + sign * mirror) * scale)
        half = g[:, freq // 2 : freq // 2 + 128]
        parts.append(jnp.where(lane == 0, (half + sign * half) * (0.5 / freq), 0.0))
        high, low = halves(join(parts, 1))
        out_ref[r] = dot(gh, high) + dot(gh, low) + dot(gl, high)
    for copy in copies[4:]:
        copy.wait()


def shifted(pair, by, inner, lane, first):
    turned = [pltpu.roll(x, by, 1).astype(F32) for x in pair]
    heads = [x[:, :128] for x in turned]
    count = heads[1].shape[0]
    step = count // inner
    last = jnp.where(first, 0.0, pltpu.roll(heads[1][count - step :], 2, 0))
    before = [join([last, heads[1][: count - step]], 0), heads[0]]
    return [join([jnp.where(lane < by, before[h], heads[h]), turned[h][:, 128:]], 1) for h in range(2)]


def main_kernel(got_ref, ghat_ref, scal_ref, w_ref, v_ref, lag_ref, out_ref):
    count, streams, mine, chunk = got_ref.shape
    sub = w_ref.shape[1]
    turns = ghat_ref.shape[1] // 2
    lags = turns // 2
    per = sub // chunk
    steps = out_ref.shape[0]
    inner = lags // steps
    rows = lags * mine
    lane = lax.broadcasted_iota(jnp.int32, (rows, 128), 1)
    first = lax.broadcasted_iota(jnp.int32, (steps * mine, 128), 0) < mine

    def spread(k):
        return jnp.tile(scal_ref[k], (rows // scal_ref.shape[1], 1))

    features = []
    for g in range(streams):
        x = got_ref[:, g].reshape(inner, per, steps * mine, chunk)
        pair = [x[:, h].reshape(rows, chunk) for h in range(per)]
        one, far = (shifted(pair, by, inner, lane, first) for by in (1, 2))
        t = [spread(3 * g + i) for i in range(3)]
        features.append(join([t[0] * pair[h].astype(F32) + t[1] * one[h] + t[2] * far[h] for h in range(per)], 1))
    query, key, value = features
    product = key * value
    high, low = halves(product)
    spec = dot(high, w_ref[0]) + dot(low, w_ref[0]) + dot(high, w_ref[1])
    spec = spec.reshape(lags, mine, 2 * sub)
    parts = []
    for r in range(mine):
        own = spec[:, r]
        parts.append(join([own[:, :sub], own[:, sub:]], 0))
    zh, zl = halves(join(parts, 1))
    wide = 2 * turns
    ahh, bhl, bh = lag_ref[:wide], lag_ref[wide : 2 * wide], lag_ref[2 * wide : 2 * wide + turns]
    al = lag_ref[2 * wide + turns :]
    al = join([al[:, :turns], al[:, turns:]], 0)
    xhat = dot(ahh, join([zh, zl], 0)) + dot(al, zh)
    parts, tails = [], []
    for r in range(mine):
        xr, xi = (xhat[k : k + turns, r * sub : (r + 1) * sub] for k in (0, turns))
        gr, gi = (ghat_ref[r, k : k + turns, :] for k in (0, turns))
        for real, imag, out, w in ((gr[:, :sub], gi[:, :sub], parts, sub), (gr[:, sub:], gi[:, sub:], tails, 128)):
            ur, ui = xr[:, :w], xi[:, :w]
            out.append(join([real * ur - imag * ui, real * ui + imag * ur], 0))
    yh, yl = halves(join(parts + tails, 1))
    both = dot(bhl, yh)
    mixed = both[:turns] + both[turns:] + dot(bh, yl)
    zero = lax.broadcasted_iota(jnp.int32, (lags, 128), 1) == 0
    parts = []
    for r in range(mine):
        real = mixed[:lags, r * sub : (r + 1) * sub]
        imag = mixed[lags:, r * sub : (r + 1) * sub]
        tail = mixed[lags:, mine * sub + r * 128 : mine * sub + (r + 1) * 128]
        parts.append(join([real, jnp.where(zero, tail, imag[:, :128]), imag[:, 128:]], 1))
    mh, ml = halves(join(parts, 0))
    long_part = dot(mh, v_ref[0]) + dot(ml, v_ref[0]) + dot(mh, v_ref[1])
    long_part = jnp.stack([long_part[r * lags : (r + 1) * lags] for r in range(mine)], axis=1).reshape(rows, sub)
    gain = jnp.tile(spread(3 * streams), (1, per))
    gated = (query * (long_part + gain * product)).astype(BF16).reshape(inner, steps, mine, sub)
    for b in range(inner):
        out_ref[:, :, b * sub : (b + 1) * sub] = gated[b]


def body(projections, taps, filter_spectra, skip_gain):
    chan_count, seq_count = lax.axis_size("chan"), lax.axis_size("seq")
    count = chan_count * seq_count
    streams, channels, tokens = projections.shape
    mine = channels // count
    length = tokens * count
    lags = filter_spectra.shape[1]
    freq = filter_spectra.shape[3]
    sub = freq // 2
    width = sub + 128
    local = filter_spectra.shape[0]
    per = sub // tokens
    inner = chan_count // per
    forward, inverse = block_tables(sub)
    order = np.arange(lags).reshape(seq_count, inner).T.reshape(-1)
    across, woven, back = lag_tables(lags, order)
    w, v = np.stack(table(forward)), np.stack(table(inverse))
    ah, al = table(across)
    bh, bl = table(back)
    woven = np.concatenate(table(woven), axis=0)
    al = np.concatenate([al[: 2 * lags], al[2 * lags :]], axis=1)
    lag = np.concatenate([np.concatenate([ah, ah], axis=1), bh, bl, bh, al], axis=0)
    vmem, hbm = pl.BlockSpec(memory_space=pltpu.VMEM), pl.BlockSpec(memory_space=pltpu.HBM)
    dma = pltpu.SemaphoreType.DMA

    sent = pl.pallas_call(
        send_kernel,
        out_shape=jax.ShapeDtypeStruct((count, streams, mine, tokens), BF16),
        in_specs=[hbm],
        out_specs=hbm,
        scratch_shapes=[
            pltpu.VMEM((streams, channels, tokens), BF16),
            pltpu.VMEM((count, streams, mine, tokens), BF16),
            dma((streams,)),
            dma,
        ],
        compiler_params=pltpu.CompilerParams(vmem_limit_bytes=8 << 20),
    )(fixed(projections))
    got = lax.all_to_all(sent, ("chan", "seq"), 0, 0, tiled=True)
    tables = w, v, lag
    ghat, scalars, *ready = pl.pallas_call(
        filter_kernel,
        out_shape=[
            jax.ShapeDtypeStruct((mine, 4 * lags, width), F32),
            jax.ShapeDtypeStruct((streams * 3 + 1, 8, tokens), F32),
        ]
        + [jax.ShapeDtypeStruct(t.shape, BF16) for t in tables],
        in_specs=[hbm] * 7,
        out_specs=[vmem] * 5,
        scratch_shapes=[
            pltpu.VMEM((mine,) + filter_spectra.shape[1:], F32),
            pltpu.VMEM((streams, taps.shape[2], channels), F32),
            pltpu.VMEM((1, channels), F32),
            pltpu.VMEM(woven.shape, BF16),
            dma((7,)),
        ],
        compiler_params=pltpu.CompilerParams(vmem_limit_bytes=12 << 20),
        cost_estimate=pl.CostEstimate(flops=1 << 28, bytes_accessed=4 << 20, transcendentals=0),
    )(*map(fixed, (filter_spectra, taps.transpose(0, 2, 1), skip_gain.reshape(1, channels), woven, *tables)))
    out = pl.pallas_call(
        main_kernel,
        out_shape=jax.ShapeDtypeStruct((seq_count, mine, length // seq_count), BF16),
        in_specs=[vmem] * 6,
        out_specs=vmem,
        compiler_params=pltpu.CompilerParams(vmem_limit_bytes=24 << 20),
        cost_estimate=pl.CostEstimate(flops=1 << 30, bytes_accessed=8 << 20, transcendentals=0),
    )(got, ghat, scalars, *ready)
    out = lax.all_to_all(out, "seq", 0, 0, tiled=True)
    return out.reshape(local, length // seq_count)


def solution(mesh):
    placed = (P(None, None, ("seq", "chan")), P(), P("chan", None, None, None), P())
    return jax.shard_map(
        body, mesh=mesh, in_specs=placed, out_specs=P("chan", "seq"), check_vma=False
    )
```

```python
import jax
import jax.numpy as jnp
import numpy as np
from jax import lax
from jax.experimental import pallas as pl
from jax.experimental.pallas import tpu as pltpu
from jax.sharding import PartitionSpec as P

F32, BF16 = jnp.float32, jnp.bfloat16


def halves(x):
    high = x.astype(BF16)
    return high, (x - high.astype(F32)).astype(BF16)


def table(x):
    high = np.asarray(x, np.float32).astype(BF16)
    low = (np.asarray(x, np.float64) - high.astype(np.float64)).astype(BF16)
    return high, low


def dot(a, b):
    return jnp.dot(a, b, preferred_element_type=F32)


def fixed(x):
    return pltpu.with_memory_space_constraint(jnp.asarray(x), pltpu.HBM)


def join(parts, axis):
    return jnp.concatenate(parts, axis=axis)


def block_tables(sub):
    freq = 2 * sub
    s = np.arange(sub)[:, None]
    f = np.arange(sub)[None, :]
    angle = 2 * np.pi * ((s * f) % freq) / freq
    imag = -np.sin(angle)
    imag[:, 0] = 1.0 - 2.0 * (np.arange(sub) % 2)
    forward = np.concatenate([np.cos(angle), imag], axis=1)
    return forward, np.ascontiguousarray(forward.T)


def lag_tables(lags, order):
    turns = 2 * lags
    k = np.arange(turns)[:, None]

    def turn(p):
        theta = 2 * np.pi * ((k * p[None, :]) % turns) / turns
        c, sn = np.cos(theta), np.sin(theta)
        return c, sn, np.block([[c, sn], [-sn, c]])

    woven = turn(np.arange(lags))[2]
    woven = woven.reshape(2 * turns, 2, lags).transpose(0, 2, 1).reshape(2 * turns, 2 * lags)
    c, sn, across = turn(order)
    back = np.block([[c.T, -sn.T], [sn.T, c.T]]) / turns
    return across, woven, back


def send_kernel(x_ref, out_ref, x_buf, out_buf, in_sem, out_sem):
    count, streams, mine, tokens = out_ref.shape
    reads = [pltpu.make_async_copy(x_ref.at[g], x_buf.at[g], in_sem.at[g]) for g in range(streams)]
    for read in reads:
        read.start()
    for g in range(streams):
        reads[g].wait()
        out_buf[:, g] = x_buf[g].reshape(count, mine, tokens)
    write = pltpu.make_async_copy(out_buf, out_ref, out_sem)
    write.start()
    write.wait()


def filter_kernel(g_hbm, taps_hbm, gain_hbm, lag_hbm, *refs):
    tables_hbm, out_ref, scal_ref, tables_ref = refs[:2], refs[2], refs[3], refs[4:6]
    g_ref, taps_ref, gain_ref, lag_ref, sems = refs[6:]
    mine, lags, two, freq = g_ref.shape
    local = g_hbm.shape[0]
    rows = lags * two
    tiles = freq // 128
    place = lax.axis_index("seq") * mine
    offset = lax.axis_index("chan") * local + place
    copies = [
        pltpu.make_async_copy(g_hbm.at[pl.ds(place, mine)], g_ref, sems.at[0]),
        pltpu.make_async_copy(lag_hbm, lag_ref, sems.at[1]),
        pltpu.make_async_copy(taps_hbm, taps_ref, sems.at[2]),
        pltpu.make_async_copy(gain_hbm, gain_ref, sems.at[3]),
    ]
    copies += [pltpu.make_async_copy(tables_hbm[k], tables_ref[k], sems.at[4 + k]) for k in range(2)]
    for copy in copies:
        copy.start()
    copies[3].wait()
    copies[2].wait()
    streams, edge_taps, channels = taps_ref.shape
    at = lax.broadcasted_iota(jnp.int32, (edge_taps, channels), 1)
    odd = lax.broadcasted_iota(jnp.int32, scal_ref.shape[1:], 0) % 2 == 1

    def pick(x, r):
        hit = lax.broadcasted_iota(jnp.int32, x.shape, 1) == offset + r
        return jnp.sum(jnp.where(hit, x, 0.0), axis=1, keepdims=True)

    for g in range(streams):
        even, second = (pick(taps_ref[g], r) for r in range(2))
        for i in range(edge_taps):
            scal_ref[g * edge_taps + i] = jnp.where(odd, second[i : i + 1], even[i : i + 1])
    even, second = (pick(gain_ref[...], r) for r in range(2))
    scal_ref[streams * edge_taps] = jnp.where(odd, second, even)

    lane = lax.broadcasted_iota(jnp.int32, (rows, 128), 1)
    row = lax.broadcasted_iota(jnp.int32, (rows, 128), 0)
    sign = jnp.where(row % 2 == 0, 1.0, -1.0).astype(F32)
    behind = (128 - lane) % 128
    copies[1].wait()
    copies[0].wait()
    wide = 2 * rows
    gh, gl = lag_ref[:wide], lag_ref[wide:]
    for r in range(mine):
        g = g_ref[r].reshape(rows, freq)
        parts = []
        for t in range(tiles // 2):
            here = g[:, t * 128 : t * 128 + 128]
            far = g[:, freq - t * 128 - 128 : freq - t * 128]
            edge = (tiles - t) % tiles
            first = g[:, edge * 128 : edge * 128 + 128]
            mirror = jnp.where(lane == 0, first, jnp.take_along_axis(far, behind, axis=1))
            scale = jnp.where((lane == 0) & (t == 0), 0.5 / freq, 1.0 / freq).astype(F32)
            parts.append((here + sign * mirror) * scale)
        half = g[:, freq // 2 : freq // 2 + 128]
        parts.append(jnp.where(lane == 0, (half + sign * half) * (0.5 / freq), 0.0))
        high, low = halves(join(parts, 1))
        out_ref[r] = dot(gh, high) + dot(gh, low) + dot(gl, high)
    for copy in copies[4:]:
        copy.wait()


def shifted(pair, by, inner, lane, first):
    turned = [pltpu.roll(x, by, 1).astype(F32) for x in pair]
    heads = [x[:, :128] for x in turned]
    count = heads[1].shape[0]
    step = count // inner
    last = jnp.where(first, 0.0, pltpu.roll(heads[1][count - step :], 2, 0))
    before = [join([last, heads[1][: count - step]], 0), heads[0]]
    return [join([jnp.where(lane < by, before[h], heads[h]), turned[h][:, 128:]], 1) for h in range(2)]


def main_kernel(got_ref, ghat_ref, scal_ref, w_ref, lag_ref, low_hbm, v_hbm, out_ref, low_ref, v_ref, sems):
    count, streams, mine, chunk = got_ref.shape
    sub = w_ref.shape[0]
    turns = ghat_ref.shape[1] // 2
    lags = turns // 2
    per = sub // chunk
    steps = out_ref.shape[0]
    inner = lags // steps
    rows = lags * mine
    copies = [pltpu.make_async_copy(low_hbm, low_ref, sems.at[0])]
    copies += [pltpu.make_async_copy(v_hbm.at[k], v_ref.at[k], sems.at[1 + k]) for k in range(2)]
    for copy in copies:
        copy.start()
    lane = lax.broadcasted_iota(jnp.int32, (rows, 128), 1)
    first = lax.broadcasted_iota(jnp.int32, (steps * mine, 128), 0) < mine

    def spread(k):
        return jnp.tile(scal_ref[k], (rows // scal_ref.shape[1], 1))

    features = []
    for g in range(streams):
        x = got_ref[:, g].reshape(inner, per, steps * mine, chunk)
        pair = [x[:, h].reshape(rows, chunk) for h in range(per)]
        one, far = (shifted(pair, by, inner, lane, first) for by in (1, 2))
        t = [spread(3 * g + i) for i in range(3)]
        features.append(join([t[0] * pair[h].astype(F32) + t[1] * one[h] + t[2] * far[h] for h in range(per)], 1))
    query, key, value = features
    product = key * value
    high, low = halves(product)
    spec = dot(high, w_ref[...]) + dot(low, w_ref[...])
    copies[0].wait()
    spec = spec + dot(high, low_ref[...])
    spec = spec.reshape(lags, mine, 2 * sub)
    parts = []
    for r in range(mine):
        own = spec[:, r]
        parts.append(join([own[:, :sub], own[:, sub:]], 0))
    zh, zl = halves(join(parts, 1))
    wide = 2 * turns
    ahh, bhl, bh = lag_ref[:wide], lag_ref[wide : 2 * wide], lag_ref[2 * wide : 2 * wide + turns]
    al = lag_ref[2 * wide + turns :]
    al = join([al[:, :turns], al[:, turns:]], 0)
    xhat = dot(ahh, join([zh, zl], 0)) + dot(al, zh)
    parts, tails = [], []
    for r in range(mine):
        xr, xi = (xhat[k : k + turns, r * sub : (r + 1) * sub] for k in (0, turns))
        gr, gi = (ghat_ref[r, k : k + turns, :] for k in (0, turns))
        for real, imag, out, w in ((gr[:, :sub], gi[:, :sub], parts, sub), (gr[:, sub:], gi[:, sub:], tails, 128)):
            ur, ui = xr[:, :w], xi[:, :w]
            out.append(join([real * ur - imag * ui, real * ui + imag * ur], 0))
    yh, yl = halves(join(parts + tails, 1))
    both = dot(bhl, yh)
    mixed = both[:turns] + both[turns:] + dot(bh, yl)
    zero = lax.broadcasted_iota(jnp.int32, (lags, 128), 1) == 0
    parts = []
    for r in range(mine):
        real = mixed[:lags, r * sub : (r + 1) * sub]
        imag = mixed[lags:, r * sub : (r + 1) * sub]
        tail = mixed[lags:, mine * sub + r * 128 : mine * sub + (r + 1) * 128]
        parts.append(join([real, jnp.where(zero, tail, imag[:, :128]), imag[:, 128:]], 1))
    mh, ml = halves(join(parts, 0))
    copies[1].wait()
    copies[2].wait()
    long_part = dot(mh, v_ref[0]) + dot(ml, v_ref[0]) + dot(mh, v_ref[1])
    long_part = jnp.stack([long_part[r * lags : (r + 1) * lags] for r in range(mine)], axis=1).reshape(rows, sub)
    gain = jnp.tile(spread(3 * streams), (1, per))
    gated = (query * (long_part + gain * product)).astype(BF16).reshape(inner, steps, mine, sub)
    for b in range(inner):
        out_ref[:, :, b * sub : (b + 1) * sub] = gated[b]


def body(projections, taps, filter_spectra, skip_gain):
    chan_count, seq_count = lax.axis_size("chan"), lax.axis_size("seq")
    count = chan_count * seq_count
    streams, channels, tokens = projections.shape
    mine = channels // count
    length = tokens * count
    lags = filter_spectra.shape[1]
    freq = filter_spectra.shape[3]
    sub = freq // 2
    width = sub + 128
    local = filter_spectra.shape[0]
    per = sub // tokens
    inner = chan_count // per
    forward, inverse = block_tables(sub)
    order = np.arange(lags).reshape(seq_count, inner).T.reshape(-1)
    across, woven, back = lag_tables(lags, order)
    wh, wl = table(forward)
    v = np.stack(table(inverse))
    ah, al = table(across)
    bh, bl = table(back)
    woven = np.concatenate(table(woven), axis=0)
    al = np.concatenate([al[: 2 * lags], al[2 * lags :]], axis=1)
    lag = np.concatenate([np.concatenate([ah, ah], axis=1), bh, bl, bh, al], axis=0)
    vmem, hbm = pl.BlockSpec(memory_space=pltpu.VMEM), pl.BlockSpec(memory_space=pltpu.HBM)
    dma = pltpu.SemaphoreType.DMA

    sent = pl.pallas_call(
        send_kernel,
        out_shape=jax.ShapeDtypeStruct((count, streams, mine, tokens), BF16),
        in_specs=[hbm],
        out_specs=hbm,
        scratch_shapes=[
            pltpu.VMEM((streams, channels, tokens), BF16),
            pltpu.VMEM((count, streams, mine, tokens), BF16),
            dma((streams,)),
            dma,
        ],
        compiler_params=pltpu.CompilerParams(vmem_limit_bytes=8 << 20),
    )(fixed(projections))
    got = lax.all_to_all(sent, ("chan", "seq"), 0, 0, tiled=True)
    tables = wh, lag
    ghat, scalars, *ready = pl.pallas_call(
        filter_kernel,
        out_shape=[
            jax.ShapeDtypeStruct((mine, 4 * lags, width), F32),
            jax.ShapeDtypeStruct((streams * 3 + 1, 8, tokens), F32),
        ]
        + [jax.ShapeDtypeStruct(t.shape, BF16) for t in tables],
        in_specs=[hbm] * 6,
        out_specs=[vmem] * 4,
        scratch_shapes=[
            pltpu.VMEM((mine,) + filter_spectra.shape[1:], F32),
            pltpu.VMEM((streams, taps.shape[2], channels), F32),
            pltpu.VMEM((1, channels), F32),
            pltpu.VMEM(woven.shape, BF16),
            dma((6,)),
        ],
        compiler_params=pltpu.CompilerParams(vmem_limit_bytes=12 << 20),
        cost_estimate=pl.CostEstimate(flops=1 << 28, bytes_accessed=4 << 20, transcendentals=0),
    )(*map(fixed, (filter_spectra, taps.transpose(0, 2, 1), skip_gain.reshape(1, channels), woven, *tables)))
    out = pl.pallas_call(
        main_kernel,
        out_shape=jax.ShapeDtypeStruct((seq_count, mine, length // seq_count), BF16),
        in_specs=[vmem] * 5 + [hbm] * 2,
        out_specs=vmem,
        scratch_shapes=[pltpu.VMEM(wl.shape, BF16), pltpu.VMEM(v.shape, BF16), dma((3,))],
        compiler_params=pltpu.CompilerParams(vmem_limit_bytes=24 << 20),
        cost_estimate=pl.CostEstimate(flops=1 << 30, bytes_accessed=8 << 20, transcendentals=0),
    )(got, ghat, scalars, *ready, fixed(wl), fixed(v))
    out = lax.all_to_all(out, "seq", 0, 0, tiled=True)
    return out.reshape(local, length // seq_count)


def solution(mesh):
    placed = (P(None, None, ("seq", "chan")), P(), P("chan", None, None, None), P())
    return jax.shard_map(
        body, mesh=mesh, in_specs=placed, out_specs=P("chan", "seq"), check_vma=False
    )
```

```python
import jax
import jax.numpy as jnp
import numpy as np
from jax import lax
from jax.experimental import pallas as pl
from jax.experimental.pallas import tpu as pltpu
from jax.sharding import PartitionSpec as P

F32, BF16 = jnp.float32, jnp.bfloat16


def halves(x):
    high = x.astype(BF16)
    return high, (x - high.astype(F32)).astype(BF16)


def table(x):
    high = np.asarray(x, np.float32).astype(BF16)
    low = (np.asarray(x, np.float64) - high.astype(np.float64)).astype(BF16)
    return high, low


def dot(a, b):
    return jnp.dot(a, b, preferred_element_type=F32)


def fixed(x):
    return pltpu.with_memory_space_constraint(jnp.asarray(x), pltpu.HBM)


def join(parts, axis):
    return jnp.concatenate(parts, axis=axis)


def block_tables(sub):
    freq = 2 * sub
    s = np.arange(sub)[:, None]
    f = np.arange(sub)[None, :]
    angle = 2 * np.pi * ((s * f) % freq) / freq
    imag = -np.sin(angle)
    imag[:, 0] = 1.0 - 2.0 * (np.arange(sub) % 2)
    forward = np.concatenate([np.cos(angle), imag], axis=1)
    return forward, np.ascontiguousarray(forward.T)


def lag_tables(lags, order):
    turns = 2 * lags
    k = np.arange(turns)[:, None]

    def turn(p):
        theta = 2 * np.pi * ((k * p[None, :]) % turns) / turns
        c, sn = np.cos(theta), np.sin(theta)
        return c, sn, np.block([[c, sn], [-sn, c]])

    woven = turn(np.arange(lags))[2]
    woven = woven.reshape(2 * turns, 2, lags).transpose(0, 2, 1).reshape(2 * turns, 2 * lags)
    c, sn, across = turn(order)
    back = np.block([[c.T, -sn.T], [sn.T, c.T]]) / turns
    return across, woven, back


def send_kernel(x_ref, out_ref, x_buf, out_buf, in_sem, out_sem):
    count, streams, mine, tokens = out_ref.shape
    pieces = in_sem.shape[0]
    share = count // pieces
    reads, writes = [], []
    for k in range(pieces):
        rows, to = pl.ds(k * share * mine, share * mine), pl.ds(k * share, share)
        reads.append(pltpu.make_async_copy(x_ref.at[:, rows], x_buf.at[:, rows], in_sem.at[k]))
        writes.append(pltpu.make_async_copy(out_buf.at[to], out_ref.at[to], out_sem.at[k]))
        reads[k].start()
    for k in range(pieces):
        reads[k].wait()
        for g in range(streams):
            part = x_buf[g, k * share * mine : (k + 1) * share * mine]
            out_buf[k * share : (k + 1) * share, g] = part.reshape(share, mine, tokens)
        writes[k].start()
    for write in writes:
        write.wait()


def filter_kernel(g_hbm, taps_hbm, gain_hbm, lag_hbm, *refs):
    tables_hbm, out_ref, scal_ref, tables_ref = refs[:2], refs[2], refs[3], refs[4:6]
    g_ref, taps_ref, gain_ref, lag_ref, sems = refs[6:]
    mine, lags, two, freq = g_ref.shape
    local = g_hbm.shape[0]
    rows = lags * two
    tiles = freq // 128
    place = lax.axis_index("seq") * mine
    offset = lax.axis_index("chan") * local + place
    copies = [
        pltpu.make_async_copy(g_hbm.at[pl.ds(place, mine)], g_ref, sems.at[0]),
        pltpu.make_async_copy(lag_hbm, lag_ref, sems.at[1]),
        pltpu.make_async_copy(taps_hbm, taps_ref, sems.at[2]),
        pltpu.make_async_copy(gain_hbm, gain_ref, sems.at[3]),
    ]
    copies += [pltpu.make_async_copy(tables_hbm[k], tables_ref[k], sems.at[4 + k]) for k in range(2)]
    for copy in copies:
        copy.start()
    copies[3].wait()
    copies[2].wait()
    streams, edge_taps, channels = taps_ref.shape
    at = lax.broadcasted_iota(jnp.int32, (edge_taps, channels), 1)
    terms = scal_ref.shape[0] // mine

    def pick(x, r):
        hit = lax.broadcasted_iota(jnp.int32, x.shape, 1) == offset + r
        return jnp.sum(jnp.where(hit, x, 0.0), axis=1, keepdims=True)

    for r in range(mine):
        for g in range(streams):
            own = pick(taps_ref[g], r)
            for i in range(edge_taps):
                scal_ref[r * terms + g * edge_taps + i] = jnp.broadcast_to(own[i : i + 1], scal_ref.shape[1:])
        scal_ref[r * terms + terms - 1] = jnp.broadcast_to(pick(gain_ref[...], r), scal_ref.shape[1:])

    lane = lax.broadcasted_iota(jnp.int32, (rows, 128), 1)
    row = lax.broadcasted_iota(jnp.int32, (rows, 128), 0)
    sign = jnp.where(row % 2 == 0, 1.0, -1.0).astype(F32)
    behind = (128 - lane) % 128
    copies[1].wait()
    copies[0].wait()
    wide = 2 * rows
    gh, gl = lag_ref[:wide], lag_ref[wide:]
    for r in range(mine):
        g = g_ref[r].reshape(rows, freq)
        parts = []
        for t in range(tiles // 2):
            here = g[:, t * 128 : t * 128 + 128]
            far = g[:, freq - t * 128 - 128 : freq - t * 128]
            edge = (tiles - t) % tiles
            first = g[:, edge * 128 : edge * 128 + 128]
            mirror = jnp.where(lane == 0, first, jnp.take_along_axis(far, behind, axis=1))
            scale = jnp.where((lane == 0) & (t == 0), 0.5 / freq, 1.0 / freq).astype(F32)
            parts.append((here + sign * mirror) * scale)
        half = g[:, freq // 2 : freq // 2 + 128]
        parts.append(jnp.where(lane == 0, (half + sign * half) * (0.5 / freq), 0.0))
        high, low = halves(join(parts, 1))
        out_ref[r] = dot(gh, high) + dot(gh, low) + dot(gl, high)
    for copy in copies[4:]:
        copy.wait()


def shifted(pair, by, inner, lane, first):
    turned = [pltpu.roll(x, by, 1).astype(F32) for x in pair]
    heads = [x[:, :128] for x in turned]
    count = heads[1].shape[0]
    step = count // inner
    last = jnp.where(first, 0.0, pltpu.roll(heads[1][count - step :], 1, 0))
    before = [join([last, heads[1][: count - step]], 0), heads[0]]
    return [join([jnp.where(lane < by, before[h], heads[h]), turned[h][:, 128:]], 1) for h in range(2)]


def main_kernel(rows_ref, ghat_ref, scal_ref, w_ref, lag_ref, v_hbm, out_ref, v_ref, sems):
    streams, mine, per, lags, chunk = rows_ref.shape
    sub = per * chunk
    turns = 2 * lags
    rows = lags * mine
    terms = scal_ref.shape[0] // mine
    step = scal_ref.shape[1]
    inner = lags // step
    copies = [pltpu.make_async_copy(v_hbm.at[k], v_ref.at[k], sems.at[k]) for k in range(2)]
    for copy in copies:
        copy.start()
    lane = lax.broadcasted_iota(jnp.int32, (lags, 128), 1)
    first = lax.broadcasted_iota(jnp.int32, (step, 128), 0) == 0

    def spread(r, k, wide):
        return jnp.tile(scal_ref[r * terms + k], (inner, wide // 128))

    def feature(g, r):
        pair = [rows_ref[g, r, h] for h in range(per)]
        one, far = (shifted(pair, by, inner, lane, first) for by in (1, 2))
        t = [spread(r, 3 * g + i, chunk) for i in range(3)]
        return [t[0] * pair[h].astype(F32) + t[1] * one[h] + t[2] * far[h] for h in range(per)]

    query, key, value = ([feature(g, r) for r in range(mine)] for g in range(streams))
    product = [[key[r][h] * value[r][h] for r in range(mine)] for h in range(per)]
    high, low = halves(join([join(x, 0) for x in product], 0))
    quarter = lax.broadcasted_iota(jnp.int32, (1, sub), 1) % 4
    even = jnp.where(quarter == 0, 1.0, jnp.where(quarter == 2, -1.0, 0.0))
    odd = jnp.where(quarter == 1, 1.0, jnp.where(quarter == 3, -1.0, 0.0))
    spec = dot(high, w_ref[0]) + dot(low, w_ref[0]) + dot(high, w_ref[1])
    ar, ai, br, bi = (spec[i : i + rows, k : k + sub] for i in (0, rows) for k in (0, sub))
    real = ar + even * br + odd * bi
    imag = ai + even * bi - odd * br
    parts = [join([x[r * lags : (r + 1) * lags] for x in (real, imag)], 0) for r in range(mine)]
    zh, zl = halves(join(parts, 1))
    wide = 2 * turns
    ahh, bhl, bh = lag_ref[:wide], lag_ref[wide : 2 * wide], lag_ref[2 * wide : 2 * wide + turns]
    al = lag_ref[2 * wide + turns :]
    al = join([al[:, :turns], al[:, turns:]], 0)
    xhat = dot(ahh, join([zh, zl], 0)) + dot(al, zh)
    parts, tails = [], []
    for r in range(mine):
        xr, xi = (xhat[k : k + turns, r * sub : (r + 1) * sub] for k in (0, turns))
        gr, gi = (ghat_ref[r, k : k + turns, :] for k in (0, turns))
        for real, imag, out, w in ((gr[:, :sub], gi[:, :sub], parts, sub), (gr[:, sub:], gi[:, sub:], tails, 128)):
            ur, ui = xr[:, :w], xi[:, :w]
            out.append(join([real * ur - imag * ui, real * ui + imag * ur], 0))
    yh, yl = halves(join(parts + tails, 1))
    both = dot(bhl, yh)
    mixed = both[:turns] + both[turns:] + dot(bh, yl)
    zero = lax.broadcasted_iota(jnp.int32, (lags, 128), 1) == 0
    parts = []
    for r in range(mine):
        real = mixed[:lags, r * sub : (r + 1) * sub]
        imag = mixed[lags:, r * sub : (r + 1) * sub]
        tail = mixed[lags:, mine * sub + r * 128 : mine * sub + (r + 1) * 128]
        parts.append(join([real, jnp.where(zero, tail, imag[:, :128]), imag[:, 128:]], 1))
    mh, ml = halves(join(parts, 0))
    for copy in copies:
        copy.wait()
    long_part = dot(mh, v_ref[0]) + dot(ml, v_ref[0]) + dot(mh, v_ref[1])
    for r in range(mine):
        direct = spread(r, terms - 1, sub) * join([product[h][r] for h in range(per)], 1)
        out_ref[r] = (join(query[r], 1) * (long_part[r * lags : (r + 1) * lags] + direct)).astype(BF16)


def body(projections, taps, filter_spectra, skip_gain):
    chan_count, seq_count = lax.axis_size("chan"), lax.axis_size("seq")
    count = chan_count * seq_count
    streams, channels, tokens = projections.shape
    mine = channels // count
    length = tokens * count
    lags = filter_spectra.shape[1]
    freq = filter_spectra.shape[3]
    sub = freq // 2
    width = sub + 128
    local = filter_spectra.shape[0]
    per = sub // tokens
    inner = chan_count // per
    forward, inverse = block_tables(sub)
    order = np.arange(lags).reshape(seq_count, inner).T.reshape(-1)
    across, woven, back = lag_tables(lags, order)
    w, v = np.stack(table(forward[:tokens])), np.stack(table(inverse))
    ah, al = table(across)
    bh, bl = table(back)
    woven = np.concatenate(table(woven), axis=0)
    al = np.concatenate([al[: 2 * lags], al[2 * lags :]], axis=1)
    lag = np.concatenate([np.concatenate([ah, ah], axis=1), bh, bl, bh, al], axis=0)
    vmem, hbm = pl.BlockSpec(memory_space=pltpu.VMEM), pl.BlockSpec(memory_space=pltpu.HBM)
    dma = pltpu.SemaphoreType.DMA

    sent = pl.pallas_call(
        send_kernel,
        out_shape=jax.ShapeDtypeStruct((count, streams, mine, tokens), BF16),
        in_specs=[hbm],
        out_specs=hbm,
        scratch_shapes=[
            pltpu.VMEM((streams, channels, tokens), BF16),
            pltpu.VMEM((count, streams, mine, tokens), BF16),
            dma((4,)),
            dma((4,)),
        ],
        compiler_params=pltpu.CompilerParams(vmem_limit_bytes=8 << 20),
    )(fixed(projections))
    got = lax.all_to_all(sent, ("chan", "seq"), 0, 0, tiled=True)
    tables = w, lag
    ghat, scalars, *ready = pl.pallas_call(
        filter_kernel,
        out_shape=[
            jax.ShapeDtypeStruct((mine, 4 * lags, width), F32),
            jax.ShapeDtypeStruct((mine * (streams * 3 + 1), 8, 128), F32),
        ]
        + [jax.ShapeDtypeStruct(t.shape, BF16) for t in tables],
        in_specs=[hbm] * 6,
        out_specs=[vmem] * 4,
        scratch_shapes=[
            pltpu.VMEM((mine,) + filter_spectra.shape[1:], F32),
            pltpu.VMEM((streams, taps.shape[2], channels), F32),
            pltpu.VMEM((1, channels), F32),
            pltpu.VMEM(woven.shape, BF16),
            dma((6,)),
        ],
        compiler_params=pltpu.CompilerParams(vmem_limit_bytes=12 << 20),
        cost_estimate=pl.CostEstimate(flops=1 << 28, bytes_accessed=4 << 20, transcendentals=0),
    )(*map(fixed, (filter_spectra, taps.transpose(0, 2, 1), skip_gain.reshape(1, channels), woven, *tables)))
    rows = got.reshape(inner, per, seq_count, streams, mine, tokens).transpose(3, 4, 1, 0, 2, 5)
    rows = rows.reshape(streams, mine, per, lags, tokens)
    out = pl.pallas_call(
        main_kernel,
        out_shape=jax.ShapeDtypeStruct((mine, lags, sub), BF16),
        in_specs=[vmem] * 5 + [hbm],
        out_specs=vmem,
        scratch_shapes=[pltpu.VMEM(v.shape, BF16), dma((2,))],
        compiler_params=pltpu.CompilerParams(vmem_limit_bytes=24 << 20),
        cost_estimate=pl.CostEstimate(flops=1 << 30, bytes_accessed=8 << 20, transcendentals=0),
    )(rows, ghat, scalars, *ready, fixed(v))
    out = out.reshape(mine, inner, seq_count, sub).transpose(2, 0, 1, 3).reshape(seq_count, mine, length // seq_count)
    out = lax.all_to_all(out, "seq", 0, 0, tiled=True)
    return out.reshape(local, length // seq_count)


def solution(mesh):
    placed = (P(None, None, ("seq", "chan")), P(), P("chan", None, None, None), P())
    return jax.shard_map(
        body, mesh=mesh, in_specs=placed, out_specs=P("chan", "seq"), check_vma=False
    )
```

```python
import jax
import jax.numpy as jnp
import numpy as np
from jax import lax
from jax.experimental import pallas as pl
from jax.experimental.pallas import tpu as pltpu
from jax.sharding import PartitionSpec as P

F32, BF16 = jnp.float32, jnp.bfloat16


def halves(x):
    high = x.astype(BF16)
    return high, (x - high.astype(F32)).astype(BF16)


def table(x):
    high = np.asarray(x, np.float32).astype(BF16)
    low = (np.asarray(x, np.float64) - high.astype(np.float64)).astype(BF16)
    return high, low


def dot(a, b):
    return jnp.dot(a, b, preferred_element_type=F32)


def fixed(x):
    return pltpu.with_memory_space_constraint(jnp.asarray(x), pltpu.HBM)


def join(parts, axis):
    return jnp.concatenate(parts, axis=axis)


def block_tables(sub):
    freq = 2 * sub
    s = np.arange(sub)[:, None]
    f = np.arange(sub)[None, :]
    angle = 2 * np.pi * ((s * f) % freq) / freq
    imag = -np.sin(angle)
    imag[:, 0] = 1.0 - 2.0 * (np.arange(sub) % 2)
    forward = np.concatenate([np.cos(angle), imag], axis=1)
    return forward, np.ascontiguousarray(forward.T)


def lag_tables(lags, order):
    turns = 2 * lags
    k = np.arange(turns)[:, None]

    def turn(p):
        theta = 2 * np.pi * ((k * p[None, :]) % turns) / turns
        c, sn = np.cos(theta), np.sin(theta)
        return c, sn, np.block([[c, sn], [-sn, c]])

    woven = turn(np.arange(lags))[2]
    woven = woven.reshape(2 * turns, 2, lags).transpose(0, 2, 1).reshape(2 * turns, 2 * lags)
    c, sn, across = turn(order)
    back = np.block([[c.T, -sn.T], [sn.T, c.T]]) / turns
    return across, woven, back


def send_kernel(x_ref, out_ref, x_buf, out_buf, in_sem, out_sem):
    count, streams, mine, tokens = out_ref.shape
    pieces = in_sem.shape[0]
    share = count // pieces
    reads, writes = [], []
    for k in range(pieces):
        rows, to = pl.ds(k * share * mine, share * mine), pl.ds(k * share, share)
        reads.append(pltpu.make_async_copy(x_ref.at[:, rows], x_buf.at[:, rows], in_sem.at[k]))
        writes.append(pltpu.make_async_copy(out_buf.at[to], out_ref.at[to], out_sem.at[k]))
        reads[k].start()
    for k in range(pieces):
        reads[k].wait()
        for g in range(streams):
            part = x_buf[g, k * share * mine : (k + 1) * share * mine]
            out_buf[k * share : (k + 1) * share, g] = part.reshape(share, mine, tokens)
        writes[k].start()
    for write in writes:
        write.wait()


def filter_kernel(g_hbm, taps_hbm, gain_hbm, lag_hbm, *refs):
    tables_hbm, out_ref, scal_ref, tables_ref = refs[:2], refs[2], refs[3], refs[4:6]
    g_ref, taps_ref, gain_ref, lag_ref, sems = refs[6:]
    mine, lags, two, freq = g_ref.shape
    local = g_hbm.shape[0]
    rows = lags * two
    tiles = freq // 128
    place = lax.axis_index("seq") * mine
    offset = lax.axis_index("chan") * local + place
    copies = [
        pltpu.make_async_copy(g_hbm.at[pl.ds(place, mine)], g_ref, sems.at[0]),
        pltpu.make_async_copy(lag_hbm, lag_ref, sems.at[1]),
        pltpu.make_async_copy(taps_hbm, taps_ref, sems.at[2]),
        pltpu.make_async_copy(gain_hbm, gain_ref, sems.at[3]),
    ]
    copies += [pltpu.make_async_copy(tables_hbm[k], tables_ref[k], sems.at[4 + k]) for k in range(2)]
    for copy in copies:
        copy.start()
    copies[3].wait()
    copies[2].wait()
    streams, edge_taps, channels = taps_ref.shape
    at = lax.broadcasted_iota(jnp.int32, (edge_taps, channels), 1)
    terms = scal_ref.shape[0] // mine

    def pick(x, r):
        hit = lax.broadcasted_iota(jnp.int32, x.shape, 1) == offset + r
        return jnp.sum(jnp.where(hit, x, 0.0), axis=1, keepdims=True)

    for r in range(mine):
        for g in range(streams):
            own = pick(taps_ref[g], r)
            for i in range(edge_taps):
                scal_ref[r * terms + g * edge_taps + i] = jnp.broadcast_to(own[i : i + 1], scal_ref.shape[1:])
        scal_ref[r * terms + terms - 1] = jnp.broadcast_to(pick(gain_ref[...], r), scal_ref.shape[1:])

    lane = lax.broadcasted_iota(jnp.int32, (rows, 128), 1)
    row = lax.broadcasted_iota(jnp.int32, (rows, 128), 0)
    sign = jnp.where(row % 2 == 0, 1.0, -1.0).astype(F32)
    behind = (128 - lane) % 128
    copies[1].wait()
    copies[0].wait()
    wide = 2 * rows
    gh, gl = lag_ref[:wide], lag_ref[wide:]
    for r in range(mine):
        g = g_ref[r].reshape(rows, freq)
        parts = []
        for t in range(tiles // 2):
            here = g[:, t * 128 : t * 128 + 128]
            far = g[:, freq - t * 128 - 128 : freq - t * 128]
            edge = (tiles - t) % tiles
            first = g[:, edge * 128 : edge * 128 + 128]
            mirror = jnp.where(lane == 0, first, jnp.take_along_axis(far, behind, axis=1))
            scale = jnp.where((lane == 0) & (t == 0), 0.5 / freq, 1.0 / freq).astype(F32)
            parts.append((here + sign * mirror) * scale)
        half = g[:, freq // 2 : freq // 2 + 128]
        parts.append(jnp.where(lane == 0, (half + sign * half) * (0.5 / freq), 0.0))
        high, low = halves(join(parts, 1))
        out_ref[r] = dot(gh, high) + dot(gh, low) + dot(gl, high)
    for copy in copies[4:]:
        copy.wait()


def shifted(pair, by, inner, lane, first):
    turned = [pltpu.roll(x, by, 1).astype(F32) for x in pair]
    heads = [x[:, :128] for x in turned]
    count = heads[1].shape[0]
    step = count // inner
    last = jnp.where(first, 0.0, pltpu.roll(heads[1][count - step :], 1, 0))
    before = [join([last, heads[1][: count - step]], 0), heads[0]]
    return [join([jnp.where(lane < by, before[h], heads[h]), turned[h][:, 128:]], 1) for h in range(2)]


def main_kernel(rows_ref, ghat_ref, scal_ref, w_ref, lag_ref, v_hbm, out_ref, v_ref, sems):
    streams, mine, per, lags, chunk = rows_ref.shape
    sub = per * chunk
    turns = 2 * lags
    rows = lags * mine
    terms = scal_ref.shape[0] // mine
    step = scal_ref.shape[1]
    inner = lags // step
    copies = [pltpu.make_async_copy(v_hbm.at[k], v_ref.at[k], sems.at[k]) for k in range(2)]
    for copy in copies:
        copy.start()
    lane = lax.broadcasted_iota(jnp.int32, (lags, 128), 1)
    first = lax.broadcasted_iota(jnp.int32, (step, 128), 0) == 0

    def spread(r, k, wide):
        return jnp.tile(scal_ref[r * terms + k], (inner, wide // 128))

    def feature(g, r):
        pair = [rows_ref[g, r, h] for h in range(per)]
        one, far = (shifted(pair, by, inner, lane, first) for by in (1, 2))
        t = [spread(r, 3 * g + i, chunk) for i in range(3)]
        return [t[0] * pair[h].astype(F32) + t[1] * one[h] + t[2] * far[h] for h in range(per)]

    query, key, value = ([feature(g, r) for r in range(mine)] for g in range(streams))
    product = [[key[r][h] * value[r][h] for r in range(mine)] for h in range(per)]
    high, low = halves(join([join(x, 0) for x in product], 0))
    quarter = lax.broadcasted_iota(jnp.int32, (1, sub), 1) % 4
    even = jnp.where(quarter == 0, 1.0, jnp.where(quarter == 2, -1.0, 0.0))
    odd = jnp.where(quarter == 1, 1.0, jnp.where(quarter == 3, -1.0, 0.0))
    spec = dot(high, w_ref[0]) + dot(low, w_ref[0]) + dot(high, w_ref[1])
    ar, ai, br, bi = (spec[i : i + rows, k : k + sub] for i in (0, rows) for k in (0, sub))
    real = ar + even * br + odd * bi
    imag = ai + even * bi - odd * br
    parts = [join([x[r * lags : (r + 1) * lags] for x in (real, imag)], 0) for r in range(mine)]
    zh, zl = halves(join(parts, 1))
    wide = 2 * turns
    ahh, bhl, bh = lag_ref[:wide], lag_ref[wide : 2 * wide], lag_ref[2 * wide : 2 * wide + turns]
    al = lag_ref[2 * wide + turns :]
    al = join([al[:, :turns], al[:, turns:]], 0)
    xhat = dot(ahh, join([zh, zl], 0)) + dot(al, zh)
    parts, tails = [], []
    for r in range(mine):
        xr, xi = (xhat[k : k + turns, r * sub : (r + 1) * sub] for k in (0, turns))
        gr, gi = (ghat_ref[r, k : k + turns, :] for k in (0, turns))
        for real, imag, out, w in ((gr[:, :sub], gi[:, :sub], parts, sub), (gr[:, sub:], gi[:, sub:], tails, 128)):
            ur, ui = xr[:, :w], xi[:, :w]
            out.append(join([real * ur - imag * ui, real * ui + imag * ur], 0))
    yh, yl = halves(join(parts + tails, 1))
    both = dot(bhl, yh)
    mixed = both[:turns] + both[turns:] + dot(bh, yl)
    zero = lax.broadcasted_iota(jnp.int32, (lags, 128), 1) == 0
    parts = []
    for r in range(mine):
        real = mixed[:lags, r * sub : (r + 1) * sub]
        imag = mixed[lags:, r * sub : (r + 1) * sub]
        tail = mixed[lags:, mine * sub + r * 128 : mine * sub + (r + 1) * 128]
        parts.append(join([real, jnp.where(zero, tail, imag[:, :128]), imag[:, 128:]], 1))
    mh, ml = halves(join(parts, 0))
    for copy in copies:
        copy.wait()
    long_part = dot(mh, v_ref[0]) + dot(ml, v_ref[0]) + dot(mh, v_ref[1])
    for r in range(mine):
        direct = spread(r, terms - 1, sub) * join([product[h][r] for h in range(per)], 1)
        gated = join(query[r], 1) * (long_part[r * lags : (r + 1) * lags] + direct)
        for b in range(inner):
            out_ref[r, :, b * sub : (b + 1) * sub] = gated[b * step : (b + 1) * step].astype(BF16)


def body(projections, taps, filter_spectra, skip_gain):
    chan_count, seq_count = lax.axis_size("chan"), lax.axis_size("seq")
    count = chan_count * seq_count
    streams, channels, tokens = projections.shape
    mine = channels // count
    length = tokens * count
    lags = filter_spectra.shape[1]
    freq = filter_spectra.shape[3]
    sub = freq // 2
    width = sub + 128
    local = filter_spectra.shape[0]
    per = sub // tokens
    inner = chan_count // per
    forward, inverse = block_tables(sub)
    order = np.arange(lags).reshape(seq_count, inner).T.reshape(-1)
    across, woven, back = lag_tables(lags, order)
    w, v = np.stack(table(forward[:tokens])), np.stack(table(inverse))
    ah, al = table(across)
    bh, bl = table(back)
    woven = np.concatenate(table(woven), axis=0)
    al = np.concatenate([al[: 2 * lags], al[2 * lags :]], axis=1)
    lag = np.concatenate([np.concatenate([ah, ah], axis=1), bh, bl, bh, al], axis=0)
    vmem, hbm = pl.BlockSpec(memory_space=pltpu.VMEM), pl.BlockSpec(memory_space=pltpu.HBM)
    dma = pltpu.SemaphoreType.DMA

    sent = pl.pallas_call(
        send_kernel,
        out_shape=jax.ShapeDtypeStruct((count, streams, mine, tokens), BF16),
        in_specs=[hbm],
        out_specs=hbm,
        scratch_shapes=[
            pltpu.VMEM((streams, channels, tokens), BF16),
            pltpu.VMEM((count, streams, mine, tokens), BF16),
            dma((4,)),
            dma((4,)),
        ],
        compiler_params=pltpu.CompilerParams(vmem_limit_bytes=8 << 20),
    )(fixed(projections))
    got = lax.all_to_all(sent, ("chan", "seq"), 0, 0, tiled=True)
    tables = w, lag
    ghat, scalars, *ready = pl.pallas_call(
        filter_kernel,
        out_shape=[
            jax.ShapeDtypeStruct((mine, 4 * lags, width), F32),
            jax.ShapeDtypeStruct((mine * (streams * 3 + 1), 8, 128), F32),
        ]
        + [jax.ShapeDtypeStruct(t.shape, BF16) for t in tables],
        in_specs=[hbm] * 6,
        out_specs=[vmem] * 4,
        scratch_shapes=[
            pltpu.VMEM((mine,) + filter_spectra.shape[1:], F32),
            pltpu.VMEM((streams, taps.shape[2], channels), F32),
            pltpu.VMEM((1, channels), F32),
            pltpu.VMEM(woven.shape, BF16),
            dma((6,)),
        ],
        compiler_params=pltpu.CompilerParams(vmem_limit_bytes=12 << 20),
        cost_estimate=pl.CostEstimate(flops=1 << 28, bytes_accessed=4 << 20, transcendentals=0),
    )(*map(fixed, (filter_spectra, taps.transpose(0, 2, 1), skip_gain.reshape(1, channels), woven, *tables)))
    rows = got.reshape(inner, per, seq_count, streams, mine, tokens).transpose(3, 4, 1, 0, 2, 5)
    rows = rows.reshape(streams, mine, per, lags, tokens)
    out = pl.pallas_call(
        main_kernel,
        out_shape=jax.ShapeDtypeStruct((mine, seq_count, length // seq_count), BF16),
        in_specs=[vmem] * 5 + [hbm],
        out_specs=vmem,
        scratch_shapes=[pltpu.VMEM(v.shape, BF16), dma((2,))],
        compiler_params=pltpu.CompilerParams(vmem_limit_bytes=24 << 20),
        cost_estimate=pl.CostEstimate(flops=1 << 30, bytes_accessed=8 << 20, transcendentals=0),
    )(rows, ghat, scalars, *ready, fixed(v))
    out = lax.all_to_all(out.transpose(1, 0, 2), "seq", 0, 0, tiled=True)
    return out.reshape(local, length // seq_count)


def solution(mesh):
    placed = (P(None, None, ("seq", "chan")), P(), P("chan", None, None, None), P())
    return jax.shard_map(
        body, mesh=mesh, in_specs=placed, out_specs=P("chan", "seq"), check_vma=False
    )
```

```python
import jax
import jax.numpy as jnp
import numpy as np
from jax import lax
from jax.experimental import pallas as pl
from jax.experimental.pallas import tpu as pltpu
from jax.sharding import PartitionSpec as P

F32, BF16 = jnp.float32, jnp.bfloat16


def halves(x):
    high = x.astype(BF16)
    return high, (x - high.astype(F32)).astype(BF16)


def table(x):
    high = np.asarray(x, np.float32).astype(BF16)
    low = (np.asarray(x, np.float64) - high.astype(np.float64)).astype(BF16)
    return high, low


def dot(a, b):
    return jnp.dot(a, b, preferred_element_type=F32)


def fixed(x):
    return pltpu.with_memory_space_constraint(jnp.asarray(x), pltpu.HBM)


def join(parts, axis):
    return jnp.concatenate(parts, axis=axis)


def block_tables(sub):
    freq = 2 * sub
    s = np.arange(sub)[:, None]
    f = np.arange(sub)[None, :]
    angle = 2 * np.pi * ((s * f) % freq) / freq
    imag = -np.sin(angle)
    imag[:, 0] = 1.0 - 2.0 * (np.arange(sub) % 2)
    forward = np.concatenate([np.cos(angle), imag], axis=1)
    return forward, np.ascontiguousarray(forward.T)


def lag_tables(lags, order):
    turns = 2 * lags
    k = np.arange(turns)[:, None]

    def turn(p):
        theta = 2 * np.pi * ((k * p[None, :]) % turns) / turns
        c, sn = np.cos(theta), np.sin(theta)
        return c, sn, np.block([[c, sn], [-sn, c]])

    woven = turn(np.arange(lags))[2]
    woven = woven.reshape(2 * turns, 2, lags).transpose(0, 2, 1).reshape(2 * turns, 2 * lags)
    c, sn, across = turn(order)
    back = np.block([[c.T, -sn.T], [sn.T, c.T]]) / turns
    return across, woven, back


def send_kernel(x_ref, out_ref, x_buf, out_buf, in_sem, out_sem):
    count, streams, mine, tokens = out_ref.shape
    pieces = in_sem.shape[0]
    share = count // pieces
    reads, writes = [], []
    for k in range(pieces):
        rows, to = pl.ds(k * share * mine, share * mine), pl.ds(k * share, share)
        reads.append(pltpu.make_async_copy(x_ref.at[:, rows], x_buf.at[:, rows], in_sem.at[k]))
        writes.append(pltpu.make_async_copy(out_buf.at[to], out_ref.at[to], out_sem.at[k]))
        reads[k].start()
    for k in range(pieces):
        reads[k].wait()
        for g in range(streams):
            part = x_buf[g, k * share * mine : (k + 1) * share * mine]
            out_buf[k * share : (k + 1) * share, g] = part.reshape(share, mine, tokens)
        writes[k].start()
    for write in writes:
        write.wait()


def filter_kernel(g_hbm, taps_hbm, gain_hbm, lag_hbm, *refs):
    tables_hbm, out_ref, scal_ref, tables_ref = refs[:2], refs[2], refs[3], refs[4:6]
    g_ref, taps_ref, gain_ref, lag_ref, sems = refs[6:]
    mine, lags, two, freq = g_ref.shape
    local = g_hbm.shape[0]
    rows = lags * two
    tiles = freq // 128
    place = lax.axis_index("seq") * mine
    offset = lax.axis_index("chan") * local + place
    copies = [
        pltpu.make_async_copy(g_hbm.at[pl.ds(place, mine)], g_ref, sems.at[0]),
        pltpu.make_async_copy(lag_hbm, lag_ref, sems.at[1]),
        pltpu.make_async_copy(taps_hbm, taps_ref, sems.at[2]),
        pltpu.make_async_copy(gain_hbm, gain_ref, sems.at[3]),
    ]
    copies += [pltpu.make_async_copy(tables_hbm[k], tables_ref[k], sems.at[4 + k]) for k in range(2)]
    for copy in copies:
        copy.start()
    copies[3].wait()
    copies[2].wait()
    streams, edge_taps, channels = taps_ref.shape
    at = lax.broadcasted_iota(jnp.int32, (edge_taps, channels), 1)
    terms = scal_ref.shape[0] // mine

    def pick(x, r):
        hit = lax.broadcasted_iota(jnp.int32, x.shape, 1) == offset + r
        return jnp.sum(jnp.where(hit, x, 0.0), axis=1, keepdims=True)

    for r in range(mine):
        for g in range(streams):
            own = pick(taps_ref[g], r)
            for i in range(edge_taps):
                scal_ref[r * terms + g * edge_taps + i] = jnp.broadcast_to(own[i : i + 1], scal_ref.shape[1:])
        scal_ref[r * terms + terms - 1] = jnp.broadcast_to(pick(gain_ref[...], r), scal_ref.shape[1:])

    lane = lax.broadcasted_iota(jnp.int32, (rows, 128), 1)
    row = lax.broadcasted_iota(jnp.int32, (rows, 128), 0)
    sign = jnp.where(row % 2 == 0, 1.0, -1.0).astype(F32)
    behind = (128 - lane) % 128
    copies[1].wait()
    copies[0].wait()
    wide = 2 * rows
    gh, gl = lag_ref[:wide], lag_ref[wide:]
    for r in range(mine):
        g = g_ref[r].reshape(rows, freq)
        parts = []
        for t in range(tiles // 2):
            here = g[:, t * 128 : t * 128 + 128]
            far = g[:, freq - t * 128 - 128 : freq - t * 128]
            edge = (tiles - t) % tiles
            first = g[:, edge * 128 : edge * 128 + 128]
            mirror = jnp.where(lane == 0, first, jnp.take_along_axis(far, behind, axis=1))
            scale = jnp.where((lane == 0) & (t == 0), 0.5 / freq, 1.0 / freq).astype(F32)
            parts.append((here + sign * mirror) * scale)
        half = g[:, freq // 2 : freq // 2 + 128]
        parts.append(jnp.where(lane == 0, (half + sign * half) * (0.5 / freq), 0.0))
        high, low = halves(join(parts, 1))
        out_ref[r] = dot(gh, high) + dot(gh, low) + dot(gl, high)
    for copy in copies[4:]:
        copy.wait()


def shifted(pair, by, inner, lane, first):
    turned = [pltpu.roll(x, by, 1).astype(F32) for x in pair]
    heads = [x[:, :128] for x in turned]
    count = heads[1].shape[0]
    step = count // inner
    last = jnp.where(first, 0.0, pltpu.roll(heads[1][count - step :], 1, 0))
    before = [join([last, heads[1][: count - step]], 0), heads[0]]
    return [join([jnp.where(lane < by, before[h], heads[h]), turned[h][:, 128:]], 1) for h in range(2)]


def main_kernel(rows_ref, ghat_ref, scal_ref, w_ref, lag_ref, v_hbm, out_ref, v_ref, sems):
    streams, mine, per, lags, chunk = rows_ref.shape
    sub = per * chunk
    turns = 2 * lags
    rows = lags * mine
    terms = scal_ref.shape[0] // mine
    step = scal_ref.shape[1]
    inner = lags // step
    copies = [pltpu.make_async_copy(v_hbm.at[k], v_ref.at[k], sems.at[k]) for k in range(2)]
    for copy in copies:
        copy.start()
    lane = lax.broadcasted_iota(jnp.int32, (lags, 128), 1)
    first = lax.broadcasted_iota(jnp.int32, (step, 128), 0) == 0

    def spread(r, k, wide):
        return jnp.tile(scal_ref[r * terms + k], (inner, wide // 128))

    def feature(g, r):
        pair = [rows_ref[g, r, h] for h in range(per)]
        one, far = (shifted(pair, by, inner, lane, first) for by in (1, 2))
        t = [spread(r, 3 * g + i, chunk) for i in range(3)]
        return [t[0] * pair[h].astype(F32) + t[1] * one[h] + t[2] * far[h] for h in range(per)]

    query, key, value = ([feature(g, r) for r in range(mine)] for g in range(streams))
    product = [[key[r][h] * value[r][h] for r in range(mine)] for h in range(per)]
    high, low = halves(join([join(x, 0) for x in product], 0))
    quarter = lax.broadcasted_iota(jnp.int32, (1, sub), 1) % 4
    even = jnp.where(quarter == 0, 1.0, jnp.where(quarter == 2, -1.0, 0.0))
    odd = jnp.where(quarter == 1, 1.0, jnp.where(quarter == 3, -1.0, 0.0))
    spec = dot(high, w_ref[0]) + dot(low, w_ref[0]) + dot(high, w_ref[1])
    ar, ai, br, bi = (spec[i : i + rows, k : k + sub] for i in (0, rows) for k in (0, sub))
    real = ar + even * br + odd * bi
    imag = ai + even * bi - odd * br
    parts = [join([x[r * lags : (r + 1) * lags] for x in (real, imag)], 0) for r in range(mine)]
    zh, zl = halves(join(parts, 1))
    wide = 2 * turns
    ahh, bhl, bh = lag_ref[:wide], lag_ref[wide : 2 * wide], lag_ref[2 * wide : 2 * wide + turns]
    al = lag_ref[2 * wide + turns :]
    al = join([al[:, :turns], al[:, turns:]], 0)
    xhat = dot(ahh, join([zh, zl], 0)) + dot(al, zh)
    parts, tails = [], []
    for r in range(mine):
        xr, xi = (xhat[k : k + turns, r * sub : (r + 1) * sub] for k in (0, turns))
        gr, gi = (ghat_ref[r, k : k + turns, :] for k in (0, turns))
        for real, imag, out, w in ((gr[:, :sub], gi[:, :sub], parts, sub), (gr[:, sub:], gi[:, sub:], tails, 128)):
            ur, ui = xr[:, :w], xi[:, :w]
            out.append(join([real * ur - imag * ui, real * ui + imag * ur], 0))
    yh, yl = halves(join(parts + tails, 1))
    both = dot(bhl, yh)
    mixed = both[:turns] + both[turns:] + dot(bh, yl)
    zero = lax.broadcasted_iota(jnp.int32, (lags, 128), 1) == 0
    parts = []
    for r in range(mine):
        real = mixed[:lags, r * sub : (r + 1) * sub]
        imag = mixed[lags:, r * sub : (r + 1) * sub]
        tail = mixed[lags:, mine * sub + r * 128 : mine * sub + (r + 1) * 128]
        parts.append(join([real, jnp.where(zero, tail, imag[:, :128]), imag[:, 128:]], 1))
    mh, ml = halves(join(parts, 0))
    copies[0].wait()
    long_part = dot(mh, v_ref[0]) + dot(ml, v_ref[0])
    copies[1].wait()
    long_part = long_part + dot(mh, v_ref[1])
    for r in range(mine):
        direct = spread(r, terms - 1, sub) * join([product[h][r] for h in range(per)], 1)
        out_ref[r] = (join(query[r], 1) * (long_part[r * lags : (r + 1) * lags] + direct)).astype(BF16)


def body(projections, taps, filter_spectra, skip_gain):
    chan_count, seq_count = lax.axis_size("chan"), lax.axis_size("seq")
    count = chan_count * seq_count
    streams, channels, tokens = projections.shape
    mine = channels // count
    length = tokens * count
    lags = filter_spectra.shape[1]
    freq = filter_spectra.shape[3]
    sub = freq // 2
    width = sub + 128
    local = filter_spectra.shape[0]
    per = sub // tokens
    inner = chan_count // per
    forward, inverse = block_tables(sub)
    order = np.arange(lags).reshape(seq_count, inner).T.reshape(-1)
    across, woven, back = lag_tables(lags, order)
    w, v = np.stack(table(forward[:tokens])), np.stack(table(inverse))
    ah, al = table(across)
    bh, bl = table(back)
    woven = np.concatenate(table(woven), axis=0)
    al = np.concatenate([al[: 2 * lags], al[2 * lags :]], axis=1)
    lag = np.concatenate([np.concatenate([ah, ah], axis=1), bh, bl, bh, al], axis=0)
    vmem, hbm = pl.BlockSpec(memory_space=pltpu.VMEM), pl.BlockSpec(memory_space=pltpu.HBM)
    dma = pltpu.SemaphoreType.DMA

    sent = pl.pallas_call(
        send_kernel,
        out_shape=jax.ShapeDtypeStruct((count, streams, mine, tokens), BF16),
        in_specs=[hbm],
        out_specs=hbm,
        scratch_shapes=[
            pltpu.VMEM((streams, channels, tokens), BF16),
            pltpu.VMEM((count, streams, mine, tokens), BF16),
            dma((4,)),
            dma((4,)),
        ],
        compiler_params=pltpu.CompilerParams(vmem_limit_bytes=8 << 20),
    )(fixed(projections))
    got = lax.all_to_all(sent, ("chan", "seq"), 0, 0, tiled=True)
    tables = w, lag
    ghat, scalars, *ready = pl.pallas_call(
        filter_kernel,
        out_shape=[
            jax.ShapeDtypeStruct((mine, 4 * lags, width), F32),
            jax.ShapeDtypeStruct((mine * (streams * 3 + 1), 8, 128), F32),
        ]
        + [jax.ShapeDtypeStruct(t.shape, BF16) for t in tables],
        in_specs=[hbm] * 6,
        out_specs=[vmem] * 4,
        scratch_shapes=[
            pltpu.VMEM((mine,) + filter_spectra.shape[1:], F32),
            pltpu.VMEM((streams, taps.shape[2], channels), F32),
            pltpu.VMEM((1, channels), F32),
            pltpu.VMEM(woven.shape, BF16),
            dma((6,)),
        ],
        compiler_params=pltpu.CompilerParams(vmem_limit_bytes=12 << 20),
        cost_estimate=pl.CostEstimate(flops=1 << 28, bytes_accessed=4 << 20, transcendentals=0),
    )(*map(fixed, (filter_spectra, taps.transpose(0, 2, 1), skip_gain.reshape(1, channels), woven, *tables)))
    rows = got.reshape(inner, per, seq_count, streams, mine, tokens).transpose(3, 4, 1, 0, 2, 5)
    rows = rows.reshape(streams, mine, per, lags, tokens)
    out = pl.pallas_call(
        main_kernel,
        out_shape=jax.ShapeDtypeStruct((mine, lags, sub), BF16),
        in_specs=[vmem] * 5 + [hbm],
        out_specs=vmem,
        scratch_shapes=[pltpu.VMEM(v.shape, BF16), dma((2,))],
        compiler_params=pltpu.CompilerParams(vmem_limit_bytes=24 << 20),
        cost_estimate=pl.CostEstimate(flops=1 << 30, bytes_accessed=8 << 20, transcendentals=0),
    )(rows, ghat, scalars, *ready, fixed(v))
    out = out.reshape(mine, inner, seq_count, sub).transpose(2, 0, 1, 3).reshape(seq_count, mine, length // seq_count)
    out = lax.all_to_all(out, "seq", 0, 0, tiled=True)
    return out.reshape(local, length // seq_count)


def solution(mesh):
    placed = (P(None, None, ("seq", "chan")), P(), P("chan", None, None, None), P())
    return jax.shard_map(
        body, mesh=mesh, in_specs=placed, out_specs=P("chan", "seq"), check_vma=False
    )
```

```python
import jax
import jax.numpy as jnp
import numpy as np
from jax import lax
from jax.experimental import pallas as pl
from jax.experimental.pallas import tpu as pltpu
from jax.sharding import PartitionSpec as P

F32, BF16 = jnp.float32, jnp.bfloat16


def halves(x):
    high = x.astype(BF16)
    return high, (x - high.astype(F32)).astype(BF16)


def table(x):
    high = np.asarray(x, np.float32).astype(BF16)
    low = (np.asarray(x, np.float64) - high.astype(np.float64)).astype(BF16)
    return high, low


def dot(a, b):
    return jnp.dot(a, b, preferred_element_type=F32)


def fixed(x):
    return pltpu.with_memory_space_constraint(jnp.asarray(x), pltpu.HBM)


def join(parts, axis):
    return jnp.concatenate(parts, axis=axis)


def block_tables(sub):
    freq = 2 * sub
    s = np.arange(sub)[:, None]
    f = np.arange(sub)[None, :]
    angle = 2 * np.pi * ((s * f) % freq) / freq
    imag = -np.sin(angle)
    imag[:, 0] = 1.0 - 2.0 * (np.arange(sub) % 2)
    forward = np.concatenate([np.cos(angle), imag], axis=1)
    return forward, np.ascontiguousarray(forward.T)


def lag_tables(lags, order):
    turns = 2 * lags
    k = np.arange(turns)[:, None]

    def turn(p):
        theta = 2 * np.pi * ((k * p[None, :]) % turns) / turns
        c, sn = np.cos(theta), np.sin(theta)
        return c, sn, np.block([[c, sn], [-sn, c]])

    woven = turn(np.arange(lags))[2]
    woven = woven.reshape(2 * turns, 2, lags).transpose(0, 2, 1).reshape(2 * turns, 2 * lags)
    c, sn, across = turn(order)
    back = np.block([[c.T, -sn.T], [sn.T, c.T]]) / turns
    return across, woven, back


def send_kernel(x_ref, out_ref, x_buf, out_buf, in_sem, out_sem):
    count, streams, mine, tokens = out_ref.shape
    pieces = in_sem.shape[0]
    share = count // pieces
    reads, writes = [], []
    for k in range(pieces):
        rows, to = pl.ds(k * share * mine, share * mine), pl.ds(k * share, share)
        reads.append(pltpu.make_async_copy(x_ref.at[:, rows], x_buf.at[:, rows], in_sem.at[k]))
        writes.append(pltpu.make_async_copy(out_buf.at[to], out_ref.at[to], out_sem.at[k]))
        reads[k].start()
    for k in range(pieces):
        reads[k].wait()
        for g in range(streams):
            part = x_buf[g, k * share * mine : (k + 1) * share * mine]
            out_buf[k * share : (k + 1) * share, g] = part.reshape(share, mine, tokens)
        writes[k].start()
    for write in writes:
        write.wait()


def filter_kernel(g_hbm, taps_hbm, gain_hbm, lag_hbm, *refs):
    tables_hbm, out_ref, scal_ref, tables_ref = refs[:2], refs[2], refs[3], refs[4:6]
    g_ref, taps_ref, gain_ref, lag_ref, sems = refs[6:]
    mine, lags, two, freq = g_ref.shape
    local = g_hbm.shape[0]
    rows = lags * two
    tiles = freq // 128
    place = lax.axis_index("seq") * mine
    offset = lax.axis_index("chan") * local + place
    copies = [
        pltpu.make_async_copy(g_hbm.at[pl.ds(place, mine)], g_ref, sems.at[0]),
        pltpu.make_async_copy(lag_hbm, lag_ref, sems.at[1]),
        pltpu.make_async_copy(taps_hbm, taps_ref, sems.at[2]),
        pltpu.make_async_copy(gain_hbm, gain_ref, sems.at[3]),
    ]
    copies += [pltpu.make_async_copy(tables_hbm[k], tables_ref[k], sems.at[4 + k]) for k in range(2)]
    for copy in copies:
        copy.start()
    copies[3].wait()
    copies[2].wait()
    streams, edge_taps, channels = taps_ref.shape
    at = lax.broadcasted_iota(jnp.int32, (edge_taps, channels), 1)
    terms = scal_ref.shape[0] // mine

    def pick(x, r):
        hit = lax.broadcasted_iota(jnp.int32, x.shape, 1) == offset + r
        return jnp.sum(jnp.where(hit, x, 0.0), axis=1, keepdims=True)

    for r in range(mine):
        for g in range(streams):
            own = pick(taps_ref[g], r)
            for i in range(edge_taps):
                scal_ref[r * terms + g * edge_taps + i] = jnp.broadcast_to(own[i : i + 1], scal_ref.shape[1:])
        scal_ref[r * terms + terms - 1] = jnp.broadcast_to(pick(gain_ref[...], r), scal_ref.shape[1:])

    lane = lax.broadcasted_iota(jnp.int32, (rows, 128), 1)
    row = lax.broadcasted_iota(jnp.int32, (rows, 128), 0)
    sign = jnp.where(row % 2 == 0, 1.0, -1.0).astype(F32)
    behind = (128 - lane) % 128
    copies[1].wait()
    copies[0].wait()
    wide = 2 * rows
    gh, gl = lag_ref[:wide], lag_ref[wide:]
    for r in range(mine):
        g = g_ref[r].reshape(rows, freq)
        parts = []
        for t in range(tiles // 2):
            here = g[:, t * 128 : t * 128 + 128]
            far = g[:, freq - t * 128 - 128 : freq - t * 128]
            edge = (tiles - t) % tiles
            first = g[:, edge * 128 : edge * 128 + 128]
            mirror = jnp.where(lane == 0, first, jnp.take_along_axis(far, behind, axis=1))
            scale = jnp.where((lane == 0) & (t == 0), 0.5 / freq, 1.0 / freq).astype(F32)
            parts.append((here + sign * mirror) * scale)
        half = g[:, freq // 2 : freq // 2 + 128]
        parts.append(jnp.where(lane == 0, (half + sign * half) * (0.5 / freq), 0.0))
        high, low = halves(join(parts, 1))
        out_ref[r] = dot(gh, high) + dot(gh, low) + dot(gl, high)
    for copy in copies[4:]:
        copy.wait()


def shifted(pair, by, inner, lane, first):
    turned = [pltpu.roll(x, by, 1).astype(F32) for x in pair]
    heads = [x[:, :128] for x in turned]
    count = heads[1].shape[0]
    step = count // inner
    last = jnp.where(first, 0.0, pltpu.roll(heads[1][count - step :], 1, 0))
    before = [join([last, heads[1][: count - step]], 0), heads[0]]
    return [join([jnp.where(lane < by, before[h], heads[h]), turned[h][:, 128:]], 1) for h in range(2)]


def main_kernel(rows_ref, ghat_ref, scal_ref, w_ref, lag_ref, v_hbm, out_ref, v_ref, sems):
    streams, mine, per, lags, chunk = rows_ref.shape
    sub = per * chunk
    turns = 2 * lags
    rows = lags * mine
    terms = scal_ref.shape[0] // mine
    step = scal_ref.shape[1]
    inner = lags // step
    copies = [pltpu.make_async_copy(v_hbm.at[k], v_ref.at[k], sems.at[k]) for k in range(2)]
    for copy in copies:
        copy.start()
    lane = lax.broadcasted_iota(jnp.int32, (lags, 128), 1)
    first = lax.broadcasted_iota(jnp.int32, (step, 128), 0) == 0

    def spread(r, k, wide):
        return jnp.tile(scal_ref[r * terms + k], (inner, wide // 128))

    def feature(g, r):
        pair = [rows_ref[g, r, h] for h in range(per)]
        one, far = (shifted(pair, by, inner, lane, first) for by in (1, 2))
        t = [spread(r, 3 * g + i, chunk) for i in range(3)]
        return [t[0] * pair[h].astype(F32) + t[1] * one[h] + t[2] * far[h] for h in range(per)]

    query, key, value = ([feature(g, r) for r in range(mine)] for g in range(streams))
    product = [[key[r][h] * value[r][h] for r in range(mine)] for h in range(per)]
    high, low = halves(join([join(x, 0) for x in product], 0))
    quarter = lax.broadcasted_iota(jnp.int32, (1, sub), 1) % 4
    even = jnp.where(quarter == 0, 1.0, jnp.where(quarter == 2, -1.0, 0.0))
    odd = jnp.where(quarter == 1, 1.0, jnp.where(quarter == 3, -1.0, 0.0))
    spec = dot(high, w_ref[0]) + dot(low, w_ref[0]) + dot(high, w_ref[1])
    ar, ai, br, bi = (spec[i : i + rows, k : k + sub] for i in (0, rows) for k in (0, sub))
    real = ar + even * br + odd * bi
    imag = ai + even * bi - odd * br
    parts = [join([x[r * lags : (r + 1) * lags] for x in (real, imag)], 0) for r in range(mine)]
    zh, zl = halves(join(parts, 1))
    wide = 2 * turns
    ahh, bhl, bh = lag_ref[:wide], lag_ref[wide : 2 * wide], lag_ref[2 * wide : 2 * wide + turns]
    al = lag_ref[2 * wide + turns :]
    al = join([al[:, :turns], al[:, turns:]], 0)
    xhat = dot(ahh, join([zh, zl], 0)) + dot(al, zh)
    parts, tails = [], []
    for r in range(mine):
        xr, xi = (xhat[k : k + turns, r * sub : (r + 1) * sub] for k in (0, turns))
        gr, gi = (ghat_ref[r, k : k + turns, :] for k in (0, turns))
        for real, imag, out, w in ((gr[:, :sub], gi[:, :sub], parts, sub), (gr[:, sub:], gi[:, sub:], tails, 128)):
            ur, ui = xr[:, :w], xi[:, :w]
            out.append(join([real * ur - imag * ui, real * ui + imag * ur], 0))
    yh, yl = halves(join(parts + tails, 1))
    both = dot(bhl, yh)
    mixed = both[:turns] + both[turns:] + dot(bh, yl)
    zero = lax.broadcasted_iota(jnp.int32, (lags, 128), 1) == 0
    parts = []
    for r in range(mine):
        real = mixed[:lags, r * sub : (r + 1) * sub]
        imag = mixed[lags:, r * sub : (r + 1) * sub]
        tail = mixed[lags:, mine * sub + r * 128 : mine * sub + (r + 1) * 128]
        parts.append(join([real, jnp.where(zero, tail, imag[:, :128]), imag[:, 128:]], 1))
    mh, ml = halves(join(parts, 0))
    copies[0].wait()
    long_part = dot(mh, v_ref[0]) + dot(ml, v_ref[0])
    copies[1].wait()
    long_part = long_part + dot(mh, v_ref[1])
    for r in range(mine):
        direct = spread(r, terms - 1, sub) * join([product[h][r] for h in range(per)], 1)
        gated = join(query[r], 1) * (long_part[r * lags : (r + 1) * lags] + direct)
        for b in range(inner):
            out_ref[r, :, b * sub : (b + 1) * sub] = gated[b * step : (b + 1) * step]


def body(projections, taps, filter_spectra, skip_gain):
    chan_count, seq_count = lax.axis_size("chan"), lax.axis_size("seq")
    count = chan_count * seq_count
    streams, channels, tokens = projections.shape
    mine = channels // count
    length = tokens * count
    lags = filter_spectra.shape[1]
    freq = filter_spectra.shape[3]
    sub = freq // 2
    width = sub + 128
    local = filter_spectra.shape[0]
    per = sub // tokens
    inner = chan_count // per
    forward, inverse = block_tables(sub)
    order = np.arange(lags).reshape(seq_count, inner).T.reshape(-1)
    across, woven, back = lag_tables(lags, order)
    w, v = np.stack(table(forward[:tokens])), np.stack(table(inverse))
    ah, al = table(across)
    bh, bl = table(back)
    woven = np.concatenate(table(woven), axis=0)
    al = np.concatenate([al[: 2 * lags], al[2 * lags :]], axis=1)
    lag = np.concatenate([np.concatenate([ah, ah], axis=1), bh, bl, bh, al], axis=0)
    vmem, hbm = pl.BlockSpec(memory_space=pltpu.VMEM), pl.BlockSpec(memory_space=pltpu.HBM)
    dma = pltpu.SemaphoreType.DMA

    sent = pl.pallas_call(
        send_kernel,
        out_shape=jax.ShapeDtypeStruct((count, streams, mine, tokens), BF16),
        in_specs=[hbm],
        out_specs=hbm,
        scratch_shapes=[
            pltpu.VMEM((streams, channels, tokens), BF16),
            pltpu.VMEM((count, streams, mine, tokens), BF16),
            dma((4,)),
            dma((4,)),
        ],
        compiler_params=pltpu.CompilerParams(vmem_limit_bytes=8 << 20),
    )(fixed(projections))
    got = lax.all_to_all(sent, ("chan", "seq"), 0, 0, tiled=True)
    tables = w, lag
    ghat, scalars, *ready = pl.pallas_call(
        filter_kernel,
        out_shape=[
            jax.ShapeDtypeStruct((mine, 4 * lags, width), F32),
            jax.ShapeDtypeStruct((mine * (streams * 3 + 1), 8, 128), F32),
        ]
        + [jax.ShapeDtypeStruct(t.shape, BF16) for t in tables],
        in_specs=[hbm] * 6,
        out_specs=[vmem] * 4,
        scratch_shapes=[
            pltpu.VMEM((mine,) + filter_spectra.shape[1:], F32),
            pltpu.VMEM((streams, taps.shape[2], channels), F32),
            pltpu.VMEM((1, channels), F32),
            pltpu.VMEM(woven.shape, BF16),
            dma((6,)),
        ],
        compiler_params=pltpu.CompilerParams(vmem_limit_bytes=12 << 20),
        cost_estimate=pl.CostEstimate(flops=1 << 28, bytes_accessed=4 << 20, transcendentals=0),
    )(*map(fixed, (filter_spectra, taps.transpose(0, 2, 1), skip_gain.reshape(1, channels), woven, *tables)))
    rows = got.reshape(inner, per, seq_count, streams, mine, tokens).transpose(3, 4, 1, 0, 2, 5)
    rows = rows.reshape(streams, mine, per, lags, tokens)
    out = pl.pallas_call(
        main_kernel,
        out_shape=jax.ShapeDtypeStruct((mine, seq_count, length // seq_count), F32),
        in_specs=[vmem] * 5 + [hbm],
        out_specs=vmem,
        scratch_shapes=[pltpu.VMEM(v.shape, BF16), dma((2,))],
        compiler_params=pltpu.CompilerParams(vmem_limit_bytes=24 << 20),
        cost_estimate=pl.CostEstimate(flops=1 << 30, bytes_accessed=8 << 20, transcendentals=0),
    )(rows, ghat, scalars, *ready, fixed(v))
    out = lax.all_to_all(out.astype(BF16).transpose(1, 0, 2), "seq", 0, 0, tiled=True)
    return out.reshape(local, length // seq_count)


def solution(mesh):
    placed = (P(None, None, ("seq", "chan")), P(), P("chan", None, None, None), P())
    return jax.shard_map(
        body, mesh=mesh, in_specs=placed, out_specs=P("chan", "seq"), check_vma=False
    )
```

```python
import jax
import jax.numpy as jnp
import numpy as np
from jax import lax
from jax.experimental import pallas as pl
from jax.experimental.pallas import tpu as pltpu
from jax.sharding import PartitionSpec as P

F32, BF16 = jnp.float32, jnp.bfloat16


def halves(x):
    high = x.astype(BF16)
    return high, (x - high.astype(F32)).astype(BF16)


def table(x):
    high = np.asarray(x, np.float32).astype(BF16)
    low = (np.asarray(x, np.float64) - high.astype(np.float64)).astype(BF16)
    return high, low


def dot(a, b):
    return jnp.dot(a, b, preferred_element_type=F32)


def fixed(x):
    return pltpu.with_memory_space_constraint(jnp.asarray(x), pltpu.HBM)


def join(parts, axis):
    return jnp.concatenate(parts, axis=axis)


def block_tables(sub):
    freq = 2 * sub
    s = np.arange(sub)[:, None]
    f = np.arange(sub)[None, :]
    angle = 2 * np.pi * ((s * f) % freq) / freq
    imag = -np.sin(angle)
    imag[:, 0] = 1.0 - 2.0 * (np.arange(sub) % 2)
    forward = np.concatenate([np.cos(angle), imag], axis=1)
    return forward, np.ascontiguousarray(forward.T)


def lag_tables(lags, order):
    turns = 2 * lags
    k = np.arange(turns)[:, None]

    def turn(p):
        theta = 2 * np.pi * ((k * p[None, :]) % turns) / turns
        c, sn = np.cos(theta), np.sin(theta)
        return c, sn, np.block([[c, sn], [-sn, c]])

    woven = turn(np.arange(lags))[2]
    woven = woven.reshape(2 * turns, 2, lags).transpose(0, 2, 1).reshape(2 * turns, 2 * lags)
    c, sn, across = turn(order)
    back = np.block([[c.T, -sn.T], [sn.T, c.T]]) / turns
    return across, woven, back


def send_kernel(x_ref, out_ref, x_buf, out_buf, in_sem, out_sem):
    count, streams, mine, tokens = out_ref.shape
    pieces = in_sem.shape[0]
    share = count // pieces
    reads, writes = [], []
    for k in range(pieces):
        rows, to = pl.ds(k * share * mine, share * mine), pl.ds(k * share, share)
        reads.append(pltpu.make_async_copy(x_ref.at[:, rows], x_buf.at[:, rows], in_sem.at[k]))
        writes.append(pltpu.make_async_copy(out_buf.at[to], out_ref.at[to], out_sem.at[k]))
        reads[k].start()
    for k in range(pieces):
        reads[k].wait()
        for g in range(streams):
            part = x_buf[g, k * share * mine : (k + 1) * share * mine]
            out_buf[k * share : (k + 1) * share, g] = part.reshape(share, mine, tokens)
        writes[k].start()
    for write in writes:
        write.wait()


def filter_kernel(g_hbm, taps_hbm, gain_hbm, lag_hbm, *refs):
    tables_hbm, out_ref, scal_ref, tables_ref = refs[:2], refs[2], refs[3], refs[4:6]
    g_ref, taps_ref, gain_ref, lag_ref, sems = refs[6:]
    mine, lags, two, freq = g_ref.shape
    local = g_hbm.shape[0]
    rows = lags * two
    tiles = freq // 128
    place = lax.axis_index("seq") * mine
    offset = lax.axis_index("chan") * local + place
    copies = [
        pltpu.make_async_copy(g_hbm.at[pl.ds(place, mine)], g_ref, sems.at[0]),
        pltpu.make_async_copy(lag_hbm, lag_ref, sems.at[1]),
        pltpu.make_async_copy(taps_hbm, taps_ref, sems.at[2]),
        pltpu.make_async_copy(gain_hbm, gain_ref, sems.at[3]),
    ]
    copies += [pltpu.make_async_copy(tables_hbm[k], tables_ref[k], sems.at[4 + k]) for k in range(2)]
    for copy in copies:
        copy.start()
    copies[3].wait()
    copies[2].wait()
    streams, edge_taps, channels = taps_ref.shape
    at = lax.broadcasted_iota(jnp.int32, (edge_taps, channels), 1)
    terms = scal_ref.shape[0] // mine

    def pick(x, r):
        hit = lax.broadcasted_iota(jnp.int32, x.shape, 1) == offset + r
        return jnp.sum(jnp.where(hit, x, 0.0), axis=1, keepdims=True)

    for r in range(mine):
        for g in range(streams):
            own = pick(taps_ref[g], r)
            for i in range(edge_taps):
                scal_ref[r * terms + g * edge_taps + i] = jnp.broadcast_to(own[i : i + 1], scal_ref.shape[1:])
        scal_ref[r * terms + terms - 1] = jnp.broadcast_to(pick(gain_ref[...], r), scal_ref.shape[1:])

    lane = lax.broadcasted_iota(jnp.int32, (rows, 128), 1)
    row = lax.broadcasted_iota(jnp.int32, (rows, 128), 0)
    sign = jnp.where(row % 2 == 0, 1.0, -1.0).astype(F32)
    behind = (128 - lane) % 128
    copies[1].wait()
    copies[0].wait()
    wide = 2 * rows
    gh, gl = lag_ref[:wide], lag_ref[wide:]
    for r in range(mine):
        g = g_ref[r].reshape(rows, freq)
        parts = []
        for t in range(tiles // 2):
            here = g[:, t * 128 : t * 128 + 128]
            far = g[:, freq - t * 128 - 128 : freq - t * 128]
            edge = (tiles - t) % tiles
            first = g[:, edge * 128 : edge * 128 + 128]
            mirror = jnp.where(lane == 0, first, jnp.take_along_axis(far, behind, axis=1))
            scale = jnp.where((lane == 0) & (t == 0), 0.5 / freq, 1.0 / freq).astype(F32)
            parts.append((here + sign * mirror) * scale)
        half = g[:, freq // 2 : freq // 2 + 128]
        parts.append(jnp.where(lane == 0, (half + sign * half) * (0.5 / freq), 0.0))
        high, low = halves(join(parts, 1))
        out_ref[r] = dot(gh, high) + dot(gh, low) + dot(gl, high)
    for copy in copies[4:]:
        copy.wait()


def shifted(pair, by, inner, lane, first):
    turned = [pltpu.roll(x, by, 1).astype(F32) for x in pair]
    heads = [x[:, :128] for x in turned]
    count = heads[1].shape[0]
    step = count // inner
    last = jnp.where(first, 0.0, pltpu.roll(heads[1][count - step :], 1, 0))
    before = [join([last, heads[1][: count - step]], 0), heads[0]]
    return [join([jnp.where(lane < by, before[h], heads[h]), turned[h][:, 128:]], 1) for h in range(2)]


def main_kernel(rows_ref, ghat_ref, scal_ref, w_ref, lag_ref, v_hbm, out_ref, v_ref, sems):
    streams, mine, per, lags, chunk = rows_ref.shape
    sub = per * chunk
    turns = 2 * lags
    rows = lags * mine
    terms = scal_ref.shape[0] // mine
    step = scal_ref.shape[1]
    inner = lags // step
    copies = [pltpu.make_async_copy(v_hbm.at[k], v_ref.at[k], sems.at[k]) for k in range(2)]
    for copy in copies:
        copy.start()
    lane = lax.broadcasted_iota(jnp.int32, (lags, 128), 1)
    first = lax.broadcasted_iota(jnp.int32, (step, 128), 0) == 0

    def spread(r, k, wide):
        return jnp.tile(scal_ref[r * terms + k], (inner, wide // 128))

    def feature(g, r):
        pair = [rows_ref[g, r, h] for h in range(per)]
        one, far = (shifted(pair, by, inner, lane, first) for by in (1, 2))
        t = [spread(r, 3 * g + i, chunk) for i in range(3)]
        return [t[0] * pair[h].astype(F32) + t[1] * one[h] + t[2] * far[h] for h in range(per)]

    query, key, value = ([feature(g, r) for r in range(mine)] for g in range(streams))
    product = [[key[r][h] * value[r][h] for r in range(mine)] for h in range(per)]
    high, low = halves(join([join(x, 0) for x in product], 0))
    quarter = lax.broadcasted_iota(jnp.int32, (1, sub), 1) % 4
    even = jnp.where(quarter == 0, 1.0, jnp.where(quarter == 2, -1.0, 0.0))
    odd = jnp.where(quarter == 1, 1.0, jnp.where(quarter == 3, -1.0, 0.0))
    spec = dot(high, w_ref[0]) + dot(low, w_ref[0]) + dot(high, w_ref[1])
    ar, ai, br, bi = (spec[i : i + rows, k : k + sub] for i in (0, rows) for k in (0, sub))
    real = ar + even * br + odd * bi
    imag = ai + even * bi - odd * br
    parts = [join([x[r * lags : (r + 1) * lags] for x in (real, imag)], 0) for r in range(mine)]
    zh, zl = halves(join(parts, 1))
    wide = 2 * turns
    ahh, bhl, bh = lag_ref[:wide], lag_ref[wide : 2 * wide], lag_ref[2 * wide : 2 * wide + turns]
    al = lag_ref[2 * wide + turns :]
    al = join([al[:, :turns], al[:, turns:]], 0)
    xhat = dot(ahh, join([zh, zl], 0)) + dot(al, zh)
    parts, tails = [], []
    for r in range(mine):
        xr, xi = (xhat[k : k + turns, r * sub : (r + 1) * sub] for k in (0, turns))
        gr, gi = (ghat_ref[r, k : k + turns, :] for k in (0, turns))
        for real, imag, out, w in ((gr[:, :sub], gi[:, :sub], parts, sub), (gr[:, sub:], gi[:, sub:], tails, 128)):
            ur, ui = xr[:, :w], xi[:, :w]
            out.append(join([real * ur - imag * ui, real * ui + imag * ur], 0))
    yh, yl = halves(join(parts + tails, 1))
    both = dot(bhl, yh)
    mixed = both[:turns] + both[turns:] + dot(bh, yl)
    zero = lax.broadcasted_iota(jnp.int32, (lags, 128), 1) == 0
    parts = []
    for r in range(mine):
        real = mixed[:lags, r * sub : (r + 1) * sub]
        imag = mixed[lags:, r * sub : (r + 1) * sub]
        tail = mixed[lags:, mine * sub + r * 128 : mine * sub + (r + 1) * 128]
        parts.append(join([real, jnp.where(zero, tail, imag[:, :128]), imag[:, 128:]], 1))
    mh, ml = halves(join(parts, 0))
    for copy in copies:
        copy.wait()
    long_part = dot(mh, v_ref[0]) + dot(ml, v_ref[0]) + dot(mh, v_ref[1])
    for r in range(mine):
        direct = spread(r, terms - 1, sub) * join([product[h][r] for h in range(per)], 1)
        out_ref[r] = (join(query[r], 1) * (long_part[r * lags : (r + 1) * lags] + direct)).astype(BF16)


def body(projections, taps, filter_spectra, skip_gain):
    chan_count, seq_count = lax.axis_size("chan"), lax.axis_size("seq")
    count = chan_count * seq_count
    streams, channels, tokens = projections.shape
    mine = channels // count
    length = tokens * count
    lags = filter_spectra.shape[1]
    freq = filter_spectra.shape[3]
    sub = freq // 2
    width = sub + 128
    local = filter_spectra.shape[0]
    per = sub // tokens
    inner = chan_count // per
    forward, inverse = block_tables(sub)
    order = np.arange(lags).reshape(seq_count, inner).T.reshape(-1)
    across, woven, back = lag_tables(lags, order)
    w, v = np.stack(table(forward[:tokens])), np.stack(table(inverse))
    ah, al = table(across)
    bh, bl = table(back)
    woven = np.concatenate(table(woven), axis=0)
    al = np.concatenate([al[: 2 * lags], al[2 * lags :]], axis=1)
    lag = np.concatenate([np.concatenate([ah, ah], axis=1), bh, bl, bh, al], axis=0)
    vmem, hbm = pl.BlockSpec(memory_space=pltpu.VMEM), pl.BlockSpec(memory_space=pltpu.HBM)
    dma = pltpu.SemaphoreType.DMA

    sent = pl.pallas_call(
        send_kernel,
        out_shape=jax.ShapeDtypeStruct((count, streams, mine, tokens), BF16),
        in_specs=[hbm],
        out_specs=hbm,
        scratch_shapes=[
            pltpu.VMEM((streams, channels, tokens), BF16),
            pltpu.VMEM((count, streams, mine, tokens), BF16),
            dma((8,)),
            dma((8,)),
        ],
        compiler_params=pltpu.CompilerParams(vmem_limit_bytes=8 << 20),
    )(fixed(projections))
    got = lax.all_to_all(sent, ("chan", "seq"), 0, 0, tiled=True)
    tables = w, lag
    ghat, scalars, *ready = pl.pallas_call(
        filter_kernel,
        out_shape=[
            jax.ShapeDtypeStruct((mine, 4 * lags, width), F32),
            jax.ShapeDtypeStruct((mine * (streams * 3 + 1), 8, 128), F32),
        ]
        + [jax.ShapeDtypeStruct(t.shape, BF16) for t in tables],
        in_specs=[hbm] * 6,
        out_specs=[vmem] * 4,
        scratch_shapes=[
            pltpu.VMEM((mine,) + filter_spectra.shape[1:], F32),
            pltpu.VMEM((streams, taps.shape[2], channels), F32),
            pltpu.VMEM((1, channels), F32),
            pltpu.VMEM(woven.shape, BF16),
            dma((6,)),
        ],
        compiler_params=pltpu.CompilerParams(vmem_limit_bytes=12 << 20),
        cost_estimate=pl.CostEstimate(flops=1 << 28, bytes_accessed=4 << 20, transcendentals=0),
    )(*map(fixed, (filter_spectra, taps.transpose(0, 2, 1), skip_gain.reshape(1, channels), woven, *tables)))
    rows = got.reshape(inner, per, seq_count, streams, mine, tokens).transpose(3, 4, 1, 0, 2, 5)
    rows = rows.reshape(streams, mine, per, lags, tokens)
    out = pl.pallas_call(
        main_kernel,
        out_shape=jax.ShapeDtypeStruct((mine, lags, sub), BF16),
        in_specs=[vmem] * 5 + [hbm],
        out_specs=vmem,
        scratch_shapes=[pltpu.VMEM(v.shape, BF16), dma((2,))],
        compiler_params=pltpu.CompilerParams(vmem_limit_bytes=24 << 20),
        cost_estimate=pl.CostEstimate(flops=1 << 30, bytes_accessed=8 << 20, transcendentals=0),
    )(rows, ghat, scalars, *ready, fixed(v))
    out = out.reshape(mine, inner, seq_count, sub).transpose(2, 0, 1, 3).reshape(seq_count, mine, length // seq_count)
    out = lax.all_to_all(out, "seq", 0, 0, tiled=True)
    return out.reshape(local, length // seq_count)


def solution(mesh):
    placed = (P(None, None, ("seq", "chan")), P(), P("chan", None, None, None), P())
    return jax.shard_map(
        body, mesh=mesh, in_specs=placed, out_specs=P("chan", "seq"), check_vma=False
    )
```
